32 devices in a mesh: seq: 4 (over y, core), fsdp: 8 (over z, x).
Axes of the slice: x: 2, y: 2, z: 4, core: 2. Of those that a mesh axis runs over, the one named last changes fastest.
Arguments:
- inputs: bfloat16 [8, 1024, 640], P('fsdp', 'seq'), may hold values from -6 to 6
- cotangent: bfloat16 [8, 1024, 640], P('fsdp', 'seq'), may hold values from -6 to 6
- query_proj: bfloat16 [640, 1024], P('fsdp'), may hold values from -0.25 to 0.25
- key_proj: bfloat16 [640, 256], P('fsdp'), may hold values from -0.25 to 0.25
- value_proj: bfloat16 [640, 256], P('fsdp'), may hold values from -0.25 to 0.25
- output_proj: bfloat16 [1024, 640], P('fsdp'), may hold values from -0.1875 to 0.1875
- gate_proj: bfloat16 [640, 2048], P('fsdp'), may hold values from -0.25 to 0.25
- up_proj: bfloat16 [640, 2048], P('fsdp'), may hold values from -0.25 to 0.25
- down_proj: bfloat16 [2048, 640], P('fsdp'), may hold values from -0.125 to 0.125
- attn_norm: bfloat16 [640], P('fsdp'), may hold values from 0.5 to 1.5
- attn_post_norm: bfloat16 [640], P('fsdp'), may hold values from 0.5 to 1.5
- ffn_norm: bfloat16 [640], P('fsdp'), may hold values from 0.5 to 1.5
- ffn_post_norm: bfloat16 [640], P('fsdp'), may hold values from 0.5 to 1.5
- query_norm: bfloat16 [256], P('fsdp'), may hold values from 0.5 to 1.5
- key_norm: bfloat16 [256], P('fsdp'), may hold values from 0.5 to 1.5
Outputs:
- outputs: bfloat16 [8, 1024, 640], P('fsdp', 'seq')
- input_grad: bfloat16 [8, 1024, 640], P('fsdp', 'seq')
- query_proj_grad: float32 [640, 1024], P('fsdp')
- key_proj_grad: float32 [640, 256], P('fsdp')
- value_proj_grad: float32 [640, 256], P('fsdp')
- output_proj_grad: float32 [1024, 640], P('fsdp')
- gate_proj_grad: float32 [640, 2048], P('fsdp')
- up_proj_grad: float32 [640, 2048], P('fsdp')
- down_proj_grad: float32 [2048, 640], P('fsdp')
- attn_norm_grad: float32 [640], P('fsdp')
- attn_post_norm_grad: float32 [640], P('fsdp')
- ffn_norm_grad: float32 [640], P('fsdp')
- ffn_post_norm_grad: float32 [640], P('fsdp')
- query_norm_grad: float32 [256], P('fsdp')
- key_norm_grad: float32 [256], P('fsdp')
The draws below stay inside these ranges and needn't reach their ends.
All inputs are finite; a program needn't handle non-finite values.
Results may differ from the reference program's by a relative error of at most 0.017.
Values may be sent and summed in bfloat16 or wider, within the bound.
A program may use at most 128 MiB of HBM per device.

```python
import math
import jax
import jax.numpy as jnp
from jax import lax

D = 640
HEADS = 4
HD = 256
FF = 2048
WINDOW = 512
SEQS = 8
LENGTH = 1024


def block_scale(key, shape, shards, low, top_value):
    factor_of = 1.0
    for dim, blocks in shards:
        steps = jax.random.uniform(jax.random.fold_in(jax.random.fold_in(key, 6), dim), (blocks,), jnp.float32, low / len(shards), top_value / len(shards))
        factor_of = factor_of * jnp.repeat(jnp.exp(steps), shape[dim] // blocks).reshape((-1,) + (1,) * (len(shape) - 1 - dim))
    return factor_of


def noise(own_key, extent, deviation, reach, shards=(), held_as=jnp.bfloat16):
    drawn = jax.random.normal(own_key, extent, jnp.float32) * deviation
    if len(shards) > 0:
        drawn = block_scale(own_key, extent, shards, -0.22, 0.18) * drawn
    return jnp.clip(drawn, min=-reach, max=reach).astype(held_as)


def setup_inputs(seed: int = 0) -> dict:
    arg_keys = jax.random.split(jax.random.key(seed), 16)
    inputs = noise(arg_keys[0], (SEQS, LENGTH, D), 1.0, 6.0, ((0, 8), (1, 4)))
    cotangent = noise(arg_keys[1], (SEQS, LENGTH, D), 1.0, 6.0, ((0, 8), (1, 4)))
    query_proj = noise(arg_keys[2], (D, HEADS * HD), D ** -0.5, 0.25, ((0, 8),))
    key_proj = noise(arg_keys[3], (D, HD), D ** -0.5, 0.25, ((0, 8),))
    value_proj = noise(arg_keys[4], (D, HD), D ** -0.5, 0.25, ((0, 8),))
    output_proj = noise(arg_keys[5], (HEADS * HD, D), (HEADS * HD) ** -0.5, 0.1875, ((0, 8),))
    gate_proj = noise(arg_keys[6], (D, FF), D ** -0.5, 0.25, ((0, 8),))
    up_proj = noise(arg_keys[7], (D, FF), D ** -0.5, 0.25, ((0, 8),))
    down_proj = noise(arg_keys[8], (FF, D), FF ** -0.5, 0.125, ((0, 8),))
    attn_norm = jnp.clip(1.0 + 0.1 * jax.random.normal(arg_keys[9], (D,), jnp.float32), 0.5, 1.5).astype(jnp.bfloat16)
    attn_post_norm = jnp.clip(1.0 + 0.1 * jax.random.normal(arg_keys[10], (D,), jnp.float32), 0.5, 1.5).astype(jnp.bfloat16)
    ffn_norm = jnp.clip(1.0 + 0.1 * jax.random.normal(arg_keys[11], (D,), jnp.float32), 0.5, 1.5).astype(jnp.bfloat16)
    ffn_post_norm = jnp.clip(1.0 + 0.1 * jax.random.normal(arg_keys[12], (D,), jnp.float32), 0.5, 1.5).astype(jnp.bfloat16)
    query_norm = jnp.clip(1.0 + 0.1 * jax.random.normal(arg_keys[13], (HD,), jnp.float32), 0.5, 1.5).astype(jnp.bfloat16)
    key_norm = jnp.clip(1.0 + 0.1 * jax.random.normal(arg_keys[14], (HD,), jnp.float32), 0.5, 1.5).astype(jnp.bfloat16)
    return dict(inputs=inputs, cotangent=cotangent, query_proj=query_proj, key_proj=key_proj, value_proj=value_proj, output_proj=output_proj, gate_proj=gate_proj, up_proj=up_proj, down_proj=down_proj, attn_norm=attn_norm, attn_post_norm=attn_post_norm, ffn_norm=ffn_norm, ffn_post_norm=ffn_post_norm, query_norm=query_norm, key_norm=key_norm)


@jax.custom_vjp
def low(v):
    return lax.optimization_barrier(v.astype(jnp.bfloat16)).astype(jnp.float32)

@jax.custom_vjp
def low_back(v):
    return v

def low_keep(v):
    return (low(v), None)

def low_pass(kept, grad):
    return (grad,)

def back_keep(v):
    return (v, None)

def back_low(kept, grad):
    return (low(grad),)
low.defvjp(low_keep, low_pass)
low_back.defvjp(back_keep, back_low)
eps = 1e-06
base_rate = 10000.0

def exact_dot(left, right):
    return jnp.dot(left, right, precision=lax.Precision.HIGHEST)

def rms_scale(value, gain):
    return value * lax.rsqrt(lax.optimization_barrier(jnp.mean(value * value, axis=-1, keepdims=True)) + eps) * gain

def rope_tables(positions, head_width):
    half_width = head_width // 2
    frequency = base_rate ** (-jnp.arange(half_width, dtype=jnp.float32) * 2.0 / head_width)
    angles = positions.astype(jnp.float32)[:, None] * frequency[None, :]
    return (jnp.cos(angles), jnp.sin(angles))

def rotate(value, cos_table, sin_table):
    half_width = value.shape[-1] // 2
    first_half = value[..., :half_width]
    second = value[..., half_width:]
    return jnp.concatenate([first_half * cos_table - second * sin_table, second * cos_table + first_half * sin_table], axis=-1)

def attend(query_rot, key_rot, values):
    length = query_rot.shape[0]
    head_width = key_rot.shape[1]
    score_scale = head_width ** (-0.5)
    block_rows = math.gcd(length, 512)
    block_count = length // block_rows
    key_padded = jnp.concatenate([jnp.zeros((WINDOW, head_width), jnp.float32), key_rot], 0)
    value_padded = jnp.concatenate([jnp.zeros((WINDOW, head_width), jnp.float32), values], 0)

    def one_block(block_index):
        row_start = block_index * block_rows
        query_block = lax.dynamic_slice_in_dim(query_rot, row_start, block_rows, 0)
        key_block = lax.dynamic_slice_in_dim(key_padded, row_start, block_rows + WINDOW, 0)
        value_block = lax.dynamic_slice_in_dim(value_padded, row_start, block_rows + WINDOW, 0)
        scores = low_back(jnp.einsum('qhd,kd->hqk', query_block, key_block, precision=lax.Precision.HIGHEST) * score_scale)
        query_pos = row_start + jnp.arange(block_rows, dtype=jnp.int32)
        key_pos = row_start - WINDOW + jnp.arange(block_rows + WINDOW, dtype=jnp.int32)
        offset = query_pos[:, None] - key_pos[None, :]
        allowed = (offset >= 0) & (offset < WINDOW) & (key_pos[None, :] >= 0)
        masked = jnp.where(allowed[None], scores, -1e+30)
        row_max = lax.optimization_barrier(jnp.max(masked, axis=-1, keepdims=True))
        raised = jnp.exp(masked - row_max)
        attn_prob = raised / lax.optimization_barrier(jnp.sum(raised, axis=-1, keepdims=True))
        return jnp.einsum('hqk,kd->qhd', low(attn_prob), value_block, precision=lax.Precision.HIGHEST)
    blocks = lax.map(jax.checkpoint(one_block), jnp.arange(block_count, dtype=jnp.int32))
    return blocks.reshape(length, -1)

def block_layer(source, params):
    query_w, key_w, value_w, output_w, gate_w, up_w, down_w, attn_gain, attn_post_gain, ffn_gain, ffn_post_gain, query_gain, key_gain = params
    length = source.shape[0]
    head_width = key_w.shape[1]
    head_count = query_w.shape[1] // head_width
    positions = jnp.arange(length, dtype=jnp.int32)
    cos_table, sin_table = rope_tables(positions, head_width)
    normed = low(rms_scale(source, attn_gain))
    query_raw = low_back(exact_dot(normed, query_w)).reshape(length, head_count, head_width)
    key_raw = low_back(exact_dot(normed, key_w))
    values = low(low_back(exact_dot(normed, value_w)))
    query_rot = low(rotate(rms_scale(query_raw, query_gain), cos_table[:, None, :], sin_table[:, None, :]))
    key_rot = low(rotate(rms_scale(key_raw, key_gain), cos_table, sin_table))
    attended = low(low_back(attend(query_rot, key_rot, values)))
    branch = low_back(exact_dot(attended, output_w))
    middle = source + rms_scale(branch, attn_post_gain)
    normed2 = low(rms_scale(middle, ffn_gain))
    gate_val = low_back(exact_dot(normed2, gate_w))
    upper = low_back(exact_dot(normed2, up_w))
    hidden = low(jax.nn.gelu(gate_val, approximate=True) * upper)
    down_out = low_back(exact_dot(hidden, down_w))
    return middle + rms_scale(down_out, ffn_post_gain)

def reference(inputs, cotangent, query_proj, key_proj, value_proj, output_proj, gate_proj, up_proj, down_proj, attn_norm, attn_post_norm, ffn_norm, ffn_post_norm, query_norm, key_norm):
    params = (query_proj.astype(jnp.float32), key_proj.astype(jnp.float32), value_proj.astype(jnp.float32), output_proj.astype(jnp.float32), gate_proj.astype(jnp.float32), up_proj.astype(jnp.float32), down_proj.astype(jnp.float32), attn_norm.astype(jnp.float32), attn_post_norm.astype(jnp.float32), ffn_norm.astype(jnp.float32), ffn_post_norm.astype(jnp.float32), query_norm.astype(jnp.float32), key_norm.astype(jnp.float32))
    source = inputs.astype(jnp.float32)

    def forward(values_in, weights):
        return lax.map(jax.checkpoint(lambda sequence: block_layer(sequence, weights)), values_in)
    result, pullback = jax.vjp(forward, source, params)
    grad_input, grad_params = pullback(cotangent.astype(jnp.float32))
    return (result.astype(jnp.bfloat16), grad_input.astype(jnp.bfloat16), grad_params[0], grad_params[1], grad_params[2], grad_params[3], grad_params[4], grad_params[5], grad_params[6], grad_params[7], grad_params[8], grad_params[9], grad_params[10], grad_params[11], grad_params[12])
```

```python
import functools

import jax
import jax.numpy as jnp
from jax import lax
from jax.experimental import pallas as pl
from jax.experimental.pallas import tpu as pltpu
from jax.sharding import PartitionSpec as P

WINDOW = 512


eps = 1e-06
base_rate = 10000.0


def shifted(array, axis, by):
    size = lax.axis_size(axis)
    pairs = [(i, i + by) for i in range(size) if 0 <= i + by < size]
    return lax.ppermute(array, axis, pairs)


def rms_scale(value, gain):
    return value * lax.rsqrt(jnp.mean(value * value, axis=-1, keepdims=True) + eps) * gain


def rope_tables(positions, head_width):
    half_width = head_width // 2
    frequency = base_rate ** (-jnp.arange(half_width, dtype=jnp.float32) * 2.0 / head_width)
    angles = positions.astype(jnp.float32)[:, None] * frequency[None, :]
    return (jnp.cos(angles), jnp.sin(angles))


def rotate(value, cos_table, sin_table):
    half_width = value.shape[-1] // 2
    first_half = value[..., :half_width]
    second = value[..., half_width:]
    return jnp.concatenate(
        [first_half * cos_table - second * sin_table, second * cos_table + first_half * sin_table],
        axis=-1,
    )


def row_outer(left, right):
    return lax.dot_general(
        left, right, (((0,), (0,)), ((), ())), preferred_element_type=jnp.float32
    )


def back_product(grad_rows, weight):
    return lax.dot_general(
        grad_rows, weight, (((1,), (1,)), ((), ())), preferred_element_type=jnp.float32
    )


MESH = pl.DeviceIdType.MESH
VMEM_BYTES = 56 * 1024 * 1024


def ring_owner(place, size):
    place = lax.rem(place + 2 * size, size)
    return jnp.where(place < size // 2, 2 * place, 2 * (size - 1 - place) + 1)


def ring_place(owner, size):
    return jnp.where(lax.rem(owner, 2) == 0, owner // 2, size - 1 - owner // 2)


def half_of(shape, by_rows, which):
    rows, columns = shape
    if by_rows:
        size = rows // 2
        return (pl.ds(pl.multiple_of(which * size, size & -size), size), slice(None))
    size = columns // 2
    return (slice(None), pl.ds(pl.multiple_of(which * size, 128), size))


def half_shape(shape, by_rows):
    rows, columns = shape
    return (rows // 2, columns) if by_rows else (rows, columns // 2)


def greet(peers):
    barrier = pltpu.get_barrier_semaphore()
    for peer in peers:
        pl.semaphore_signal(barrier, inc=1, device_id=peer, device_id_type=MESH)
    pl.semaphore_wait(barrier, len(peers))


def gather_kernel(size, shapes, by_rows, *refs):
    count = len(shapes)
    shards, gains = refs[:count], refs[count]
    wholes, all_gains = refs[count + 1 : 2 * count + 1], refs[2 * count + 1]
    own_sem, ring_send, ring_recv, pair_send, pair_recv = refs[2 * count + 2 :]
    seq, me = lax.axis_index("seq"), lax.axis_index("fsdp")
    core = lax.rem(seq, 2)
    way = 1 - 2 * core
    place = ring_place(me, size)
    after = (seq, ring_owner(place + way, size))
    before = (seq, ring_owner(place - way, size))
    pair = (seq + way, me)
    greet([after, before, pair])

    def ring_copy(member, block, step, first=False):
        if member == count:
            source, target = gains if first else all_gains.at[block], all_gains.at[block]
        else:
            part = half_of(shapes[member], by_rows[member], core)
            target = wholes[member].at[(block, *part)]
            source = shards[member].at[part] if first else target
        return pltpu.make_async_remote_copy(
            src_ref=source,
            dst_ref=target,
            send_sem=ring_send.at[step, member],
            recv_sem=ring_recv.at[step, member],
            device_id=after,
            device_id_type=MESH,
        )

    def pair_copy(member, block, step, which):
        part = half_of(shapes[member], by_rows[member], which)
        target = wholes[member].at[(block, *part)]
        return pltpu.make_async_remote_copy(
            src_ref=target,
            dst_ref=target,
            send_sem=pair_send.at[step, member],
            recv_sem=pair_recv.at[step, member],
            device_id=pair,
            device_id_type=MESH,
        )

    own = []
    for member in range(count + 1):
        ring_copy(member, me, 0, first=True).start()
    for member in range(count):
        own.append(
            pltpu.make_async_copy(shards[member], wholes[member].at[me], own_sem.at[member])
        )
    own.append(pltpu.make_async_copy(gains, all_gains.at[me], own_sem.at[count]))
    for copy in own:
        copy.start()

    def arrive(step, forward):
        block = ring_owner(place - way * step, size)
        for member in range(count + 1):
            ring_copy(member, block, step - 1).wait_recv()
            if forward:
                ring_copy(member, block, step).start()
            if member < count:
                pair_copy(member, block, step - 1, core).start()

    lax.fori_loop(1, size - 1, lambda step, _: (arrive(step, True), 0)[1], 0)
    arrive(size - 1, False)
    for copy in own:
        copy.wait()

    def finish(step, _):
        for member in range(count + 1):
            ring_copy(member, me, step).wait_send()
            if member < count:
                pair_copy(member, me, step, core).wait_send()
                block = ring_owner(place + way * (step + 1), size)
                pair_copy(member, block, step, 1 - core).wait_recv()
        return 0

    lax.fori_loop(0, size - 1, finish, 0)


def gather_weights(shards, by_rows, gains):
    size = lax.axis_size("fsdp")
    shapes = [shard.shape for shard in shards]
    count = len(shards)
    any_space = pl.BlockSpec(memory_space=pl.ANY)
    copies = pltpu.SemaphoreType.DMA((size - 1, count + 1))
    return pl.pallas_call(
        functools.partial(gather_kernel, size, shapes, by_rows),
        out_shape=[
            jax.ShapeDtypeStruct((size, *member.shape), member.dtype) for member in (*shards, gains)
        ],
        in_specs=[any_space] * (count + 1),
        out_specs=[any_space] * (count + 1),
        scratch_shapes=[pltpu.SemaphoreType.DMA((count + 1,)), copies, copies, copies, copies],
        compiler_params=pltpu.CompilerParams(collective_id=0, has_side_effects=True),
        name="gather_weights",
    )(*shards, gains)


def reduce_kernel(size, blocks, shapes, by_rows, *refs):
    count = len(shapes)
    every = list(refs)

    def take(number):
        taken = every[:number]
        del every[:number]
        return taken

    mine, (gain_mine,) = take(count), take(1)
    totals, (gain_total,) = take(count), take(1)
    parts, landed, spread = take(count), take(count), take(count)
    gain_sent, gain_landed, gain_spread = take(3)
    pair_send, pair_recv, ring_send, ring_recv = take(4)
    spread_send, spread_recv, gain_send, gain_recv, last_send, last_recv = take(6)

    seq, me = lax.axis_index("seq"), lax.axis_index("fsdp")
    core = lax.rem(seq, 2)
    row = seq // 2
    rows = blocks // 2
    way = 1 - 2 * core
    place = ring_place(me, size)
    after = (seq, ring_owner(place + way, size))
    before = (seq, ring_owner(place - way, size))
    pair = (seq + way, me)
    others = [(lax.rem(seq + by, blocks), me) for by in range(1, blocks)]
    greet([after, before, *others])

    def remote(source, target, send_sem, recv_sem, device):
        return pltpu.make_async_remote_copy(
            src_ref=source,
            dst_ref=target,
            send_sem=send_sem,
            recv_sem=recv_sem,
            device_id=device,
            device_id_type=MESH,
        )

    def pair_copy(member, step):
        block = ring_owner(place + way * (1 + step), size)
        part = half_of(shapes[member], by_rows[member], 1 - core)
        return remote(
            mine[member].at[(block, *part)],
            parts[member].at[block],
            pair_send.at[step, member],
            pair_recv.at[step, member],
            pair,
        )

    def ring_copy(member, step):
        block = ring_owner(place - way * (1 + step), size)
        source = gain_sent.at[step] if member == count else parts[member].at[block]
        target = gain_landed.at[step] if member == count else landed[member].at[step]
        return remote(
            source, target, ring_send.at[step, member], ring_recv.at[step, member], after
        )

    def start_pair(step, _):
        for member in range(count):
            pair_copy(member, step).start()
        return 0

    lax.fori_loop(0, size, start_pair, 0)

    def add_up(step, first, last):
        block = ring_owner(place - way * (1 + step), size)
        for member in range(count):
            pair_copy(member, step).wait_recv()
            part = half_of(shapes[member], by_rows[member], core)
            total = mine[member][(block, *part)].astype(jnp.float32)
            total = total + parts[member][block].astype(jnp.float32)
            if not first:
                ring_copy(member, step - 1).wait_recv()
                total = total + landed[member][step - 1].astype(jnp.float32)
            if last:
                spread[member][row] = total.astype(jnp.bfloat16)
                for by in range(1, rows):
                    spread_copy(member, by).start()
            else:
                parts[member][block] = total.astype(jnp.bfloat16)
                ring_copy(member, step).start()
        total = gain_mine[block]
        if not first:
            ring_copy(count, step - 1).wait_recv()
            total = total + gain_landed[step - 1]
        if last:
            gain_spread[seq] = total
            for by in range(1, blocks):
                gain_copy(by).start()
        else:
            gain_sent[step] = total
            ring_copy(count, step).start()

    def spread_copy(member, by):
        target = spread[member].at[row]
        device = (lax.rem(seq + 2 * by, blocks), me)
        return remote(
            target, target, spread_send.at[by - 1, member], spread_recv.at[by - 1, member], device
        )

    def gain_copy(by):
        target = gain_spread.at[seq]
        return remote(
            target, target, gain_send.at[by - 1], gain_recv.at[by - 1], others[by - 1]
        )

    def last_copy(member):
        target = totals[member].at[half_of(shapes[member], by_rows[member], core)]
        return remote(target, target, last_send.at[member], last_recv.at[member], pair)

    add_up(0, True, False)
    lax.fori_loop(1, size - 1, lambda step, _: (add_up(step, False, False), 0)[1], 0)
    add_up(size - 1, False, True)
    for member in range(count):
        for by in range(1, rows):
            spread_copy(member, by).wait_recv()
        total = spread[member][0].astype(jnp.float32)
        for other in range(1, rows):
            total = total + spread[member][other].astype(jnp.float32)
        totals[member][half_of(shapes[member], by_rows[member], core)] = total
        last_copy(member).start()
    for by in range(1, blocks):
        gain_copy(by).wait_recv()
    total = gain_spread[0]
    for other in range(1, blocks):
        total = total + gain_spread[other]
    gain_total[...] = total

    def finish(step, _):
        for member in range(count + 1):
            ring_copy(member, step).wait_send()
        return 0

    lax.fori_loop(0, size - 1, finish, 0)

    def finish_pair(step, _):
        for member in range(count):
            pair_copy(member, step).wait_send()
        return 0

    lax.fori_loop(0, size, finish_pair, 0)
    for member in range(count):
        for by in range(1, rows):
            spread_copy(member, by).wait_send()
        last_copy(member).wait()
    for by in range(1, blocks):
        gain_copy(by).wait_send()


def reduce_grads(grads, by_rows, gain_grads):
    size, blocks = lax.axis_size("fsdp"), lax.axis_size("seq")
    shapes = [grad.shape[1:] for grad in grads]
    halves = [half_shape(*both) for both in zip(shapes, by_rows)]
    count = len(grads)
    gain_shape = gain_grads.shape[1:]
    rows = blocks // 2
    in_vmem = pl.BlockSpec(memory_space=pltpu.VMEM)
    dma = pltpu.SemaphoreType.DMA
    return pl.pallas_call(
        functools.partial(reduce_kernel, size, blocks, shapes, by_rows),
        out_shape=[jax.ShapeDtypeStruct(shape, jnp.float32) for shape in (*shapes, gain_shape)],
        in_specs=[in_vmem] * (count + 1),
        out_specs=[in_vmem] * (count + 1),
        scratch_shapes=[
            *[pltpu.VMEM((size, *half), jnp.bfloat16) for half in halves],
            *[pltpu.VMEM((size - 1, *half), jnp.bfloat16) for half in halves],
            *[pltpu.VMEM((rows, *half), jnp.bfloat16) for half in halves],
            pltpu.VMEM((size - 1, *gain_shape), jnp.float32),
            pltpu.VMEM((size - 1, *gain_shape), jnp.float32),
            pltpu.VMEM((blocks, *gain_shape), jnp.float32),
            dma((size, count)),
            dma((size, count)),
            dma((size - 1, count + 1)),
            dma((size - 1, count + 1)),
            dma((rows, count)),
            dma((rows, count)),
            dma((blocks,)),
            dma((blocks,)),
            dma((count,)),
            dma((count,)),
        ],
        compiler_params=pltpu.CompilerParams(
            collective_id=1, has_side_effects=True, vmem_limit_bytes=VMEM_BYTES
        ),
        name="reduce_grads",
    )(*grads, gain_grads)


def pack_gains(members, rows, split):
    row = jnp.concatenate([member.reshape(*split, -1) for member in members], axis=-1)
    padding = -row.shape[-1] % 128
    row = jnp.pad(row, [(0, 0)] * len(split) + [(0, padding)])
    return jnp.broadcast_to(row[..., None, :], (*split, rows, row.shape[-1]))


def unpack_gains(rows, widths):
    pieces, start = [], 0
    for width in widths:
        pieces.append(rows[..., start : start + width])
        start += width
    return pieces


def on_device(
    inputs,
    cotangent,
    query_proj,
    key_proj,
    value_proj,
    output_proj,
    gate_proj,
    up_proj,
    down_proj,
    attn_norm,
    attn_post_norm,
    ffn_norm,
    ffn_post_norm,
    query_norm,
    key_norm,
):
    size = lax.axis_size("fsdp")
    shards = (
        jnp.concatenate([query_proj, key_proj, value_proj], axis=1),
        output_proj,
        jnp.concatenate([gate_proj, up_proj], axis=1),
        down_proj,
    )
    by_rows = (False, True, False, True)
    gain_shards = (attn_norm, attn_post_norm, ffn_norm, ffn_post_norm, query_norm, key_norm)
    widths = [member.shape[0] for member in gain_shards]
    *wholes, all_gains = gather_weights(shards, by_rows, pack_gains(gain_shards, 16, ()))
    into_w, output_w, ffn_w, down_w = (whole.reshape(-1, whole.shape[-1]) for whole in wholes)
    query_width, head_width = query_proj.shape[1], key_proj.shape[1]
    ffn_width = gate_proj.shape[1]
    attn_gain, attn_post_gain, ffn_gain, ffn_post_gain, query_gain, key_gain = (
        piece.reshape(-1).astype(jnp.float32) for piece in unpack_gains(all_gains[:, 0], widths)
    )
    source = inputs[0].astype(jnp.float32)
    tokens = source.shape[0]
    head_count = query_width // head_width
    score_scale = head_width ** (-0.5)
    hop_count = min((WINDOW + tokens - 2) // tokens, lax.axis_size("seq") - 1)
    seq_place = lax.axis_index("seq")
    positions = seq_place * tokens + jnp.arange(tokens, dtype=jnp.int32)
    cos_table, sin_table = rope_tables(positions, head_width)
    normed = rms_scale(source, attn_gain).astype(jnp.bfloat16)
    raw = jnp.dot(normed, into_w, preferred_element_type=jnp.float32)
    query_raw = raw[:, :query_width]
    key_raw = raw[:, query_width : query_width + head_width]
    value_raw = raw[:, query_width + head_width :]

    def turn_norm(query_in, key_in, q_gain, k_gain):
        query_out = rotate(
            rms_scale(query_in.reshape(tokens, head_count, head_width), q_gain),
            cos_table[:, None, :],
            sin_table[:, None, :],
        )
        key_out = rotate(rms_scale(key_in, k_gain), cos_table, sin_table)
        return (query_out, key_out)

    query_rot, key_rot = turn_norm(query_raw, key_raw, query_gain, key_gain)
    query_low = query_rot.astype(jnp.bfloat16)
    own_pairs = jnp.concatenate(
        [key_rot.astype(jnp.bfloat16), value_raw.astype(jnp.bfloat16)], axis=1
    )
    received = []
    for distance in range(1, hop_count + 1):
        received.append(shifted(own_pairs, "seq", distance))
    key_value = jnp.concatenate(received[::-1] + [own_pairs], axis=0)
    keys_ext = key_value[:, :head_width]
    values_ext = key_value[:, head_width:]
    ext_rows = key_value.shape[0]
    key_pos = (seq_place - hop_count) * tokens + jnp.arange(ext_rows, dtype=jnp.int32)
    offset = positions[:, None] - key_pos[None, :]
    allowed = ((offset >= 0) & (offset < WINDOW) & (key_pos[None, :] >= 0))[None]
    scores = (
        jnp.einsum("qhd,kd->hqk", query_low, keys_ext, preferred_element_type=jnp.float32)
        * score_scale
    )
    masked = jnp.where(allowed, scores, -1e30)
    row_max = jnp.max(masked, axis=-1, keepdims=True)
    raised = jnp.exp(masked - row_max)
    row_sum = jnp.sum(raised, axis=-1, keepdims=True)
    attn_prob = raised / row_sum
    log_total = row_max + jnp.log(row_sum)
    attended = jnp.einsum(
        "hqk,kd->qhd",
        attn_prob.astype(jnp.bfloat16),
        values_ext,
        preferred_element_type=jnp.float32,
    )
    att_low = attended.reshape(tokens, head_count * head_width).astype(jnp.bfloat16)
    branch = jnp.dot(att_low, output_w, preferred_element_type=jnp.float32)
    middle = source + rms_scale(branch, attn_post_gain)
    normed2 = rms_scale(middle, ffn_gain).astype(jnp.bfloat16)
    both = jnp.dot(normed2, ffn_w, preferred_element_type=jnp.float32)
    gate_val, upper = both[:, :ffn_width], both[:, ffn_width:]

    def act_piece(gate_in, upper_in):
        return jax.nn.gelu(gate_in, approximate=True) * upper_in

    hidden = act_piece(gate_val, upper).astype(jnp.bfloat16)
    down_out = jnp.dot(hidden, down_w, preferred_element_type=jnp.float32)
    result = middle + rms_scale(down_out, ffn_post_gain)
    grad_y = cotangent[0].astype(jnp.float32)
    _, back_post2 = jax.vjp(rms_scale, down_out, ffn_post_gain)
    grad_down, grad_post2 = back_post2(grad_y)
    grad_down_low = grad_down.astype(jnp.bfloat16)
    down_grad = row_outer(hidden, grad_down_low)
    grad_hidden = back_product(grad_down_low, down_w)
    _, back_act = jax.vjp(act_piece, gate_val, upper)
    grad_gate, grad_up = back_act(grad_hidden)
    grad_both = jnp.concatenate(
        [grad_gate.astype(jnp.bfloat16), grad_up.astype(jnp.bfloat16)], axis=1
    )
    ffn_grad = row_outer(normed2, grad_both)
    grad_normed2 = back_product(grad_both, ffn_w)
    _, back_pre2 = jax.vjp(rms_scale, middle, ffn_gain)
    grad_mid_norm, grad_pre2 = back_pre2(grad_normed2)
    grad_mid = grad_y + grad_mid_norm
    _, back_post1 = jax.vjp(rms_scale, branch, attn_post_gain)
    grad_branch, grad_post1 = back_post1(grad_mid)
    grad_branch_low = grad_branch.astype(jnp.bfloat16)
    output_grad = row_outer(att_low, grad_branch_low)
    grad_att = (
        back_product(grad_branch_low, output_w)
        .astype(jnp.bfloat16)
        .reshape(tokens, head_count, head_width)
    )
    scores_again = (
        jnp.einsum("qhd,kd->hqk", query_low, keys_ext, preferred_element_type=jnp.float32)
        * score_scale
    )
    prob_again = jnp.exp(jnp.where(allowed, scores_again, -1e30) - log_total)
    grad_prob = jnp.einsum("qhd,kd->hqk", grad_att, values_ext, preferred_element_type=jnp.float32)
    inner_sum = jnp.sum(prob_again * grad_prob, axis=-1, keepdims=True)
    grad_scores = (prob_again * (grad_prob - inner_sum)).astype(jnp.bfloat16)
    grad_query = (
        jnp.einsum("hqk,kd->qhd", grad_scores, keys_ext, preferred_element_type=jnp.float32)
        * score_scale
    )
    grad_keys_ext = (
        jnp.einsum("hqk,qhd->kd", grad_scores, query_low, preferred_element_type=jnp.float32)
        * score_scale
    )
    grad_values_ext = jnp.einsum(
        "hqk,qhd->kd", prob_again.astype(jnp.bfloat16), grad_att, preferred_element_type=jnp.float32
    )
    grad_pairs = jnp.concatenate([grad_keys_ext, grad_values_ext], axis=1)
    own_grad = grad_pairs[hop_count * tokens :]
    for distance in range(1, hop_count + 1):
        lower_row = (hop_count - distance) * tokens
        own_grad = own_grad + shifted(grad_pairs[lower_row : lower_row + tokens], "seq", -distance)
    _, back_turn = jax.vjp(turn_norm, query_raw, key_raw, query_gain, key_gain)
    grad_qraw, grad_kraw, grad_qgain, grad_kgain = back_turn((grad_query, own_grad[:, :head_width]))
    grad_raw = jnp.concatenate(
        [
            grad_qraw.astype(jnp.bfloat16),
            grad_kraw.astype(jnp.bfloat16),
            own_grad[:, head_width:].astype(jnp.bfloat16),
        ],
        axis=1,
    )
    into_grad = row_outer(normed, grad_raw)
    grad_normed = back_product(grad_raw, into_w)
    _, back_pre1 = jax.vjp(rms_scale, source, attn_gain)
    grad_source, grad_pre1 = back_pre1(grad_normed)
    grad_input = grad_mid + grad_source
    grads = [
        grad.astype(jnp.bfloat16).reshape(size, -1, grad.shape[-1])
        for grad in (into_grad, output_grad, ffn_grad, down_grad)
    ]
    gain_grads = pack_gains(
        (grad_pre1, grad_post1, grad_pre2, grad_post2, grad_qgain, grad_kgain), 8, (size,)
    )
    into_total, output_total, ffn_total, down_total, gain_total = reduce_grads(
        grads, by_rows, gain_grads
    )
    return (
        result.astype(jnp.bfloat16)[None],
        grad_input.astype(jnp.bfloat16)[None],
        into_total[:, :query_width],
        into_total[:, query_width : query_width + head_width],
        into_total[:, query_width + head_width :],
        output_total,
        ffn_total[:, :ffn_width],
        ffn_total[:, ffn_width:],
        down_total,
        *unpack_gains(gain_total[0], widths),
    )


def solution(mesh):
    placed = (
        P("fsdp", "seq", None),
        P("fsdp", "seq", None),
        P("fsdp", None),
        P("fsdp", None),
        P("fsdp", None),
        P("fsdp", None),
        P("fsdp", None),
        P("fsdp", None),
        P("fsdp", None),
        P("fsdp"),
        P("fsdp"),
        P("fsdp"),
        P("fsdp"),
        P("fsdp"),
        P("fsdp"),
    )
    return jax.shard_map(
        on_device,
        mesh=mesh,
        in_specs=placed,
        out_specs=(
            P("fsdp", "seq", None),
            P("fsdp", "seq", None),
            P("fsdp", None),
            P("fsdp", None),
            P("fsdp", None),
            P("fsdp", None),
            P("fsdp", None),
            P("fsdp", None),
            P("fsdp", None),
            P("fsdp"),
            P("fsdp"),
            P("fsdp"),
            P("fsdp"),
            P("fsdp"),
            P("fsdp"),
        ),
        check_vma=False,
    )
```

```python
import functools

import jax
import jax.numpy as jnp
from jax import lax
from jax.experimental import pallas as pl
from jax.experimental.pallas import tpu as pltpu
from jax.sharding import PartitionSpec as P

WINDOW = 512


eps = 1e-06
base_rate = 10000.0


def shifted(array, axis, by):
    size = lax.axis_size(axis)
    pairs = [(i, i + by) for i in range(size) if 0 <= i + by < size]
    return lax.ppermute(array, axis, pairs)


def rms_scale(value, gain):
    return value * lax.rsqrt(jnp.mean(value * value, axis=-1, keepdims=True) + eps) * gain


def rope_tables(positions, head_width):
    half_width = head_width // 2
    frequency = base_rate ** (-jnp.arange(half_width, dtype=jnp.float32) * 2.0 / head_width)
    angles = positions.astype(jnp.float32)[:, None] * frequency[None, :]
    return (jnp.cos(angles), jnp.sin(angles))


def rotate(value, cos_table, sin_table):
    half_width = value.shape[-1] // 2
    first_half = value[..., :half_width]
    second = value[..., half_width:]
    return jnp.concatenate(
        [first_half * cos_table - second * sin_table, second * cos_table + first_half * sin_table],
        axis=-1,
    )


def row_outer(left, right):
    return lax.dot_general(
        left, right, (((0,), (0,)), ((), ())), preferred_element_type=jnp.float32
    )


def back_product(grad_rows, weight):
    return lax.dot_general(
        grad_rows, weight, (((1,), (1,)), ((), ())), preferred_element_type=jnp.float32
    )


MESH = pl.DeviceIdType.MESH
VMEM_BYTES = 56 * 1024 * 1024


def ring_owner(place, size):
    place = lax.rem(place + 2 * size, size)
    return jnp.where(place < size // 2, 2 * place, 2 * (size - 1 - place) + 1)


def ring_place(owner, size):
    return jnp.where(lax.rem(owner, 2) == 0, owner // 2, size - 1 - owner // 2)


def region(shape, by_rows, core, plane=None):
    size = shape[0 if by_rows else 1] // 2
    start = core * size
    if plane is not None:
        size = size // 2
        start = start + plane * size
    if by_rows:
        return (pl.ds(pl.multiple_of(start, size & -size), size), slice(None))
    return (slice(None), pl.ds(pl.multiple_of(start, 128), size))


def region_shape(shape, by_rows, cuts):
    rows, columns = shape
    return (rows // cuts, columns) if by_rows else (rows, columns // cuts)


def greet(peers):
    barrier = pltpu.get_barrier_semaphore()
    for peer in peers:
        pl.semaphore_signal(barrier, inc=1, device_id=peer, device_id_type=MESH)
    pl.semaphore_wait(barrier, len(peers))


def gather_kernel(size, shapes, by_rows, shared, places, *refs):
    count = len(shapes)
    shards, gains = refs[: len(places)], refs[len(places)]
    refs = refs[len(places) + 1 :]
    wholes, all_gains = refs[:count], refs[count]
    own_sem, ring_send, ring_recv, pair_send, pair_recv = refs[count + 1 : count + 6]
    cross_send, cross_recv, relay_send, relay_recv = refs[count + 6 :]
    seq, me = lax.axis_index("seq"), lax.axis_index("fsdp")
    core, plane = lax.rem(seq, 2), lax.rem(seq // 2, 2)
    way = 1 - 2 * core
    place = ring_place(me, size)
    after = (seq, ring_owner(place + way, size))
    before = (seq, ring_owner(place - way, size))
    pair = (seq + way, me)
    across = (seq + 2 * (1 - 2 * plane), me)

    own = []
    for shard, (member, column) in zip(shards, places):
        target = wholes[member].at[me, :, pl.ds(column, shard.shape[1])]
        own.append(pltpu.make_async_copy(shard, target, own_sem.at[len(own)]))
    own.append(pltpu.make_async_copy(gains, all_gains.at[me], own_sem.at[len(own)]))
    for copy in own:
        copy.start()
    greet([after, before, pair, across])

    def copy_of(member, block, core, plane, sems, step, device):
        if member == count:
            target = all_gains.at[block]
        else:
            part = region(shapes[member], by_rows[member], core, plane)
            target = wholes[member].at[(block, *part)]
        return pltpu.make_async_remote_copy(
            src_ref=target,
            dst_ref=target,
            send_sem=sems[0].at[step, member],
            recv_sem=sems[1].at[step, member],
            device_id=device,
            device_id_type=MESH,
        )

    def plane_of(member):
        return plane if member < count and shared[member] else None

    def ring_copy(member, block, step):
        return copy_of(member, block, core, plane_of(member), (ring_send, ring_recv), step, after)

    def pair_copy(member, block, step, core):
        return copy_of(member, block, core, plane_of(member), (pair_send, pair_recv), step, pair)

    def cross_copy(member, block, step, plane):
        return copy_of(member, block, core, plane, (cross_send, cross_recv), step, across)

    def relay_copy(member, block, step, core):
        return copy_of(member, block, core, 1 - plane, (relay_send, relay_recv), step, pair)

    for copy in own:
        copy.wait()
    for member in range(count + 1):
        ring_copy(member, me, 0).start()

    def arrive(step, forward):
        block = ring_owner(place - way * step, size)
        for member in range(count + 1):
            ring_copy(member, block, step - 1).wait_recv()
            if forward:
                ring_copy(member, block, step).start()
            if member < count:
                if shared[member]:
                    cross_copy(member, block, step - 1, plane).start()
                pair_copy(member, block, step - 1, core).start()

    def relay(step):
        block = ring_owner(place - way * step, size)
        for member in range(count):
            if shared[member]:
                cross_copy(member, block, step - 1, 1 - plane).wait_recv()
                relay_copy(member, block, step - 1, core).start()

    arrive(1, True)

    def turn(step, _):
        arrive(step, True)
        relay(step - 1)
        return 0

    lax.fori_loop(2, size - 1, turn, 0)
    arrive(size - 1, False)
    relay(size - 2)
    relay(size - 1)

    def finish(step, _):
        block = ring_owner(place + way * (step + 1), size)
        for member in range(count + 1):
            ring_copy(member, me, step).wait_send()
            if member < count:
                pair_copy(member, me, step, core).wait_send()
                pair_copy(member, block, step, 1 - core).wait_recv()
                if shared[member]:
                    cross_copy(member, me, step, plane).wait_send()
                    relay_copy(member, me, step, core).wait_send()
                    relay_copy(member, block, step, 1 - core).wait_recv()
        return 0

    lax.fori_loop(0, size - 1, finish, 0)


def gather_weights(shards, groups, by_rows, shared, gains):
    size = lax.axis_size("fsdp")
    shapes, places = [], []
    for number, group in enumerate(groups):
        column = 0
        for member in group:
            places.append((number, column))
            column += shards[member].shape[1]
        shapes.append((shards[group[0]].shape[0], column))
    count = len(groups)
    any_space = pl.BlockSpec(memory_space=pl.ANY)
    copies = pltpu.SemaphoreType.DMA((size - 1, count + 1))
    return pl.pallas_call(
        functools.partial(gather_kernel, size, shapes, by_rows, shared, places),
        out_shape=[
            jax.ShapeDtypeStruct((size, *shape), gains.dtype) for shape in (*shapes, gains.shape)
        ],
        in_specs=[any_space] * (len(shards) + 1),
        out_specs=[any_space] * (count + 1),
        scratch_shapes=[pltpu.SemaphoreType.DMA((len(shards) + 1,)), *[copies] * 8],
        compiler_params=pltpu.CompilerParams(collective_id=0, has_side_effects=True),
        name="gather_weights",
    )(*shards, gains)


def reduce_kernel(size, blocks, shapes, by_rows, shared, places, *refs):
    count = len(shapes)
    every = list(refs)

    def take(number):
        taken = every[:number]
        del every[:number]
        return taken

    mine, (gain_mine,) = take(count), take(1)
    results, (gain_total,) = take(len(places)), take(1)
    totals, parts, landed, crossed = take(count), take(count), take(count), take(count)
    spread, agreed = take(count), take(count)
    gain_sent, gain_landed, gain_spread = take(3)
    pair_send, pair_recv, ring_send, ring_recv, cross_send, cross_recv = take(6)
    spread_send, spread_recv, gain_send, gain_recv = take(4)
    agree_send, agree_recv, last_send, last_recv = take(4)

    seq, me = lax.axis_index("seq"), lax.axis_index("fsdp")
    core, plane = lax.rem(seq, 2), lax.rem(seq // 2, 2)
    way = 1 - 2 * core
    place = ring_place(me, size)
    after = (seq, ring_owner(place + way, size))
    before = (seq, ring_owner(place - way, size))
    pair = (seq + way, me)
    across = (seq + 2 * (1 - 2 * plane), me)
    others = [(lax.rem(seq + by, blocks), me) for by in range(1, blocks)]
    greet([after, before, *others])

    def remote(source, target, sems, index, device):
        return pltpu.make_async_remote_copy(
            src_ref=source,
            dst_ref=target,
            send_sem=sems[0].at[index],
            recv_sem=sems[1].at[index],
            device_id=device,
            device_id_type=MESH,
        )

    def block_at(step):
        return ring_owner(place - way * (1 + step), size)

    def within(member, part):
        shape = region_shape(shapes[member], by_rows[member], 2)
        return region(shape, by_rows[member], part)

    def ring_part(member):
        return within(member, plane) if shared[member] else (slice(None), slice(None))

    def own_part(member, part):
        return region(shapes[member], by_rows[member], core, part if shared[member] else None)

    def pair_copy(member, step):
        block = ring_owner(place + way * (1 + step), size)
        part = region(shapes[member], by_rows[member], 1 - core)
        return remote(
            mine[member].at[(block, *part)],
            parts[member].at[block],
            (pair_send, pair_recv),
            (step, member),
            pair,
        )

    def ring_copy(member, step):
        if member == count:
            source, target = gain_sent.at[step], gain_landed.at[step]
        else:
            source = parts[member].at[(block_at(step), *ring_part(member))]
            target = landed[member].at[step]
        return remote(source, target, (ring_send, ring_recv), (step, member), after)

    def cross_copy(member, step):
        source = parts[member].at[(block_at(step), *within(member, 1 - plane))]
        return remote(
            source, crossed[member].at[step], (cross_send, cross_recv), (step, member), across
        )

    def start_pair(step, _):
        for member in range(count):
            pair_copy(member, step).start()
        return 0

    lax.fori_loop(0, size, start_pair, 0)

    def prepare(step):
        block = block_at(step)
        for member in range(count):
            pair_copy(member, step).wait_recv()
            if shared[member]:
                spot = (block, *within(member, 1 - plane))
                total = mine[member][(block, *own_part(member, 1 - plane))].astype(jnp.float32)
                total = total + parts[member][spot].astype(jnp.float32)
                parts[member][spot] = total.astype(jnp.bfloat16)
                cross_copy(member, step).start()

    def add_up(step, first, last):
        block = block_at(step)
        for member in range(count):
            spot = (block, *ring_part(member))
            total = mine[member][(block, *own_part(member, plane))].astype(jnp.float32)
            total = total + parts[member][spot].astype(jnp.float32)
            if shared[member]:
                cross_copy(member, step).wait_recv()
                total = total + crossed[member][step].astype(jnp.float32)
            if not first:
                ring_copy(member, step - 1).wait_recv()
                total = total + landed[member][step - 1].astype(jnp.float32)
            if last:
                spread[member][row_of(member)] = total.astype(jnp.bfloat16)
                for by in range(1, rows_of(member)):
                    spread_copy(member, by).start()
            else:
                parts[member][spot] = total.astype(jnp.bfloat16)
                ring_copy(member, step).start()
        total = gain_mine[block]
        if not first:
            ring_copy(count, step - 1).wait_recv()
            total = total + gain_landed[step - 1]
        if last:
            gain_spread[seq] = total
            for by in range(1, blocks):
                gain_copy(by).start()
        else:
            gain_sent[step] = total
            ring_copy(count, step).start()

    def stride_of(member):
        return 4 if shared[member] else 2

    def row_of(member):
        return seq // stride_of(member)

    def rows_of(member):
        return blocks // stride_of(member)

    def spread_copy(member, by):
        target = spread[member].at[row_of(member)]
        device = (lax.rem(seq + stride_of(member) * by, blocks), me)
        return remote(target, target, (spread_send, spread_recv), (by - 1, member), device)

    def gain_copy(by):
        target = gain_spread.at[seq]
        return remote(target, target, (gain_send, gain_recv), by - 1, others[by - 1])

    def agree_copy(member):
        target = agreed[member].at[within(member, plane)]
        return remote(target, target, (agree_send, agree_recv), member, across)

    def last_copy(member):
        target = totals[member].at[region(shapes[member], by_rows[member], core)]
        return remote(target, target, (last_send, last_recv), member, pair)

    prepare(0)
    prepare(1)
    add_up(0, True, False)

    def turn(step, _):
        prepare(step + 1)
        add_up(step, False, False)
        return 0

    lax.fori_loop(1, size - 1, turn, 0)
    add_up(size - 1, False, True)
    order = sorted(range(count), key=lambda member: not shared[member])
    for member in order:
        for by in range(1, rows_of(member)):
            spread_copy(member, by).wait_recv()
        total = spread[member][0].astype(jnp.float32)
        for other in range(1, rows_of(member)):
            total = total + spread[member][other].astype(jnp.float32)
        if shared[member]:
            agreed[member][within(member, plane)] = total.astype(jnp.bfloat16)
            agree_copy(member).start()
        else:
            totals[member][region(shapes[member], by_rows[member], core)] = total
            last_copy(member).start()
    for member in order:
        if shared[member]:
            agree_copy(member).wait_recv()
            total = agreed[member][...].astype(jnp.float32)
            totals[member][region(shapes[member], by_rows[member], core)] = total
            last_copy(member).start()
    for by in range(1, blocks):
        gain_copy(by).wait_recv()
    total = gain_spread[0]
    for other in range(1, blocks):
        total = total + gain_spread[other]
    gain_total[...] = total

    def finish(step, _):
        for member in range(count + 1):
            ring_copy(member, step).wait_send()
        return 0

    lax.fori_loop(0, size - 1, finish, 0)

    def finish_pair(step, _):
        for member in range(count):
            pair_copy(member, step).wait_send()
            if shared[member]:
                cross_copy(member, step).wait_send()
        return 0

    lax.fori_loop(0, size, finish_pair, 0)
    for member in range(count):
        for by in range(1, rows_of(member)):
            spread_copy(member, by).wait_send()
        if shared[member]:
            agree_copy(member).wait_send()
        last_copy(member).wait()
    for by in range(1, blocks):
        gain_copy(by).wait_send()
    for result, (member, column) in zip(results, places):
        result[...] = totals[member][:, column : column + result.shape[1]]


def reduce_grads(grads, widths, by_rows, shared, gain_grads):
    size, blocks = lax.axis_size("fsdp"), lax.axis_size("seq")
    shapes = [grad.shape[1:] for grad in grads]
    count = len(grads)
    halves = [region_shape(shapes[m], by_rows[m], 2) for m in range(count)]
    pieces = [region_shape(shapes[m], by_rows[m], 4 if shared[m] else 2) for m in range(count)]
    places, results = [], []
    for member in range(count):
        column = 0
        for width in widths[member]:
            places.append((member, column))
            results.append((shapes[member][0], width))
            column += width
    gain_shape = gain_grads.shape[1:]
    in_vmem = pl.BlockSpec(memory_space=pltpu.VMEM)
    dma = pltpu.SemaphoreType.DMA
    unused = (16, 128)

    def buffers(lengths, extents):
        return [
            pltpu.VMEM((*length, *extent), jnp.bfloat16)
            for length, extent in zip(lengths, extents)
        ]

    return pl.pallas_call(
        functools.partial(reduce_kernel, size, blocks, shapes, by_rows, shared, places),
        out_shape=[jax.ShapeDtypeStruct(shape, jnp.float32) for shape in (*results, gain_shape)],
        in_specs=[in_vmem] * (count + 1),
        out_specs=[in_vmem] * (len(results) + 1),
        scratch_shapes=[
            *[pltpu.VMEM(shape, jnp.float32) for shape in shapes],
            *buffers([(size,)] * count, halves),
            *buffers([(size - 1,)] * count, pieces),
            *buffers(
                [(size,) if member else () for member in shared],
                [pieces[m] if shared[m] else unused for m in range(count)],
            ),
            *buffers([(blocks // (4 if member else 2),) for member in shared], pieces),
            *buffers([()] * count, [halves[m] if shared[m] else unused for m in range(count)]),
            pltpu.VMEM((size - 1, *gain_shape), jnp.float32),
            pltpu.VMEM((size - 1, *gain_shape), jnp.float32),
            pltpu.VMEM((blocks, *gain_shape), jnp.float32),
            dma((size, count)),
            dma((size, count)),
            dma((size - 1, count + 1)),
            dma((size - 1, count + 1)),
            dma((size, count)),
            dma((size, count)),
            dma((blocks // 2, count)),
            dma((blocks // 2, count)),
            dma((blocks,)),
            dma((blocks,)),
            dma((count,)),
            dma((count,)),
            dma((count,)),
            dma((count,)),
        ],
        compiler_params=pltpu.CompilerParams(
            collective_id=1, has_side_effects=True, vmem_limit_bytes=VMEM_BYTES
        ),
        name="reduce_grads",
    )(*grads, gain_grads)


def pack_gains(members, rows, split):
    row = jnp.concatenate([member.reshape(*split, -1) for member in members], axis=-1)
    padding = -row.shape[-1] % 128
    row = jnp.pad(row, [(0, 0)] * len(split) + [(0, padding)])
    return jnp.broadcast_to(row[..., None, :], (*split, rows, row.shape[-1]))


def unpack_gains(rows, widths):
    pieces, start = [], 0
    for width in widths:
        pieces.append(rows[..., start : start + width])
        start += width
    return pieces


def on_device(
    inputs,
    cotangent,
    query_proj,
    key_proj,
    value_proj,
    output_proj,
    gate_proj,
    up_proj,
    down_proj,
    attn_norm,
    attn_post_norm,
    ffn_norm,
    ffn_post_norm,
    query_norm,
    key_norm,
):
    size = lax.axis_size("fsdp")
    shards = (query_proj, key_proj, value_proj, output_proj, gate_proj, up_proj, down_proj)
    groups = ((0, 1, 2), (3,), (4, 5), (6,))
    by_rows = (False, True, False, True)
    shared = (False, True, True, False)
    gain_shards = (attn_norm, attn_post_norm, ffn_norm, ffn_post_norm, query_norm, key_norm)
    widths = [member.shape[0] for member in gain_shards]
    *wholes, all_gains = gather_weights(
        shards, groups, by_rows, shared, pack_gains(gain_shards, 16, ())
    )
    into_w, output_w, ffn_w, down_w = (whole.reshape(-1, whole.shape[-1]) for whole in wholes)
    query_width, head_width = query_proj.shape[1], key_proj.shape[1]
    ffn_width = gate_proj.shape[1]
    attn_gain, attn_post_gain, ffn_gain, ffn_post_gain, query_gain, key_gain = (
        piece.reshape(-1).astype(jnp.float32) for piece in unpack_gains(all_gains[:, 0], widths)
    )
    source = inputs[0].astype(jnp.float32)
    tokens = source.shape[0]
    head_count = query_width // head_width
    score_scale = head_width ** (-0.5)
    hop_count = min((WINDOW + tokens - 2) // tokens, lax.axis_size("seq") - 1)
    seq_place = lax.axis_index("seq")
    positions = seq_place * tokens + jnp.arange(tokens, dtype=jnp.int32)
    cos_table, sin_table = rope_tables(positions, head_width)
    normed = rms_scale(source, attn_gain).astype(jnp.bfloat16)
    raw = jnp.dot(normed, into_w, preferred_element_type=jnp.float32)
    query_raw = raw[:, :query_width]
    key_raw = raw[:, query_width : query_width + head_width]
    value_raw = raw[:, query_width + head_width :]

    def turn_norm(query_in, key_in, q_gain, k_gain):
        query_out = rotate(
            rms_scale(query_in.reshape(tokens, head_count, head_width), q_gain),
            cos_table[:, None, :],
            sin_table[:, None, :],
        )
        key_out = rotate(rms_scale(key_in, k_gain), cos_table, sin_table)
        return (query_out, key_out)

    query_rot, key_rot = turn_norm(query_raw, key_raw, query_gain, key_gain)
    query_low = query_rot.astype(jnp.bfloat16)
    own_pairs = jnp.concatenate(
        [key_rot.astype(jnp.bfloat16), value_raw.astype(jnp.bfloat16)], axis=1
    )
    received = []
    for distance in range(1, hop_count + 1):
        received.append(shifted(own_pairs, "seq", distance))
    key_value = jnp.concatenate(received[::-1] + [own_pairs], axis=0)
    keys_ext = key_value[:, :head_width]
    values_ext = key_value[:, head_width:]
    ext_rows = key_value.shape[0]
    key_pos = (seq_place - hop_count) * tokens + jnp.arange(ext_rows, dtype=jnp.int32)
    offset = positions[:, None] - key_pos[None, :]
    allowed = ((offset >= 0) & (offset < WINDOW) & (key_pos[None, :] >= 0))[None]
    scores = (
        jnp.einsum("qhd,kd->hqk", query_low, keys_ext, preferred_element_type=jnp.float32)
        * score_scale
    )
    masked = jnp.where(allowed, scores, -1e30)
    row_max = jnp.max(masked, axis=-1, keepdims=True)
    raised = jnp.exp(masked - row_max)
    row_sum = jnp.sum(raised, axis=-1, keepdims=True)
    attn_prob = raised / row_sum
    log_total = row_max + jnp.log(row_sum)
    attended = jnp.einsum(
        "hqk,kd->qhd",
        attn_prob.astype(jnp.bfloat16),
        values_ext,
        preferred_element_type=jnp.float32,
    )
    att_low = attended.reshape(tokens, head_count * head_width).astype(jnp.bfloat16)
    branch = jnp.dot(att_low, output_w, preferred_element_type=jnp.float32)
    middle = source + rms_scale(branch, attn_post_gain)
    normed2 = rms_scale(middle, ffn_gain).astype(jnp.bfloat16)
    both = jnp.dot(normed2, ffn_w, preferred_element_type=jnp.float32)
    gate_val, upper = both[:, :ffn_width], both[:, ffn_width:]

    def act_piece(gate_in, upper_in):
        return jax.nn.gelu(gate_in, approximate=True) * upper_in

    hidden = act_piece(gate_val, upper).astype(jnp.bfloat16)
    down_out = jnp.dot(hidden, down_w, preferred_element_type=jnp.float32)
    result = middle + rms_scale(down_out, ffn_post_gain)
    grad_y = cotangent[0].astype(jnp.float32)
    _, back_post2 = jax.vjp(rms_scale, down_out, ffn_post_gain)
    grad_down, grad_post2 = back_post2(grad_y)
    grad_down_low = grad_down.astype(jnp.bfloat16)
    down_grad = row_outer(hidden, grad_down_low)
    grad_hidden = back_product(grad_down_low, down_w)
    _, back_act = jax.vjp(act_piece, gate_val, upper)
    grad_gate, grad_up = back_act(grad_hidden)
    grad_both = jnp.concatenate(
        [grad_gate.astype(jnp.bfloat16), grad_up.astype(jnp.bfloat16)], axis=1
    )
    ffn_grad = row_outer(normed2, grad_both)
    grad_normed2 = back_product(grad_both, ffn_w)
    _, back_pre2 = jax.vjp(rms_scale, middle, ffn_gain)
    grad_mid_norm, grad_pre2 = back_pre2(grad_normed2)
    grad_mid = grad_y + grad_mid_norm
    _, back_post1 = jax.vjp(rms_scale, branch, attn_post_gain)
    grad_branch, grad_post1 = back_post1(grad_mid)
    grad_branch_low = grad_branch.astype(jnp.bfloat16)
    output_grad = row_outer(att_low, grad_branch_low)
    grad_att = (
        back_product(grad_branch_low, output_w)
        .astype(jnp.bfloat16)
        .reshape(tokens, head_count, head_width)
    )
    scores_again = (
        jnp.einsum("qhd,kd->hqk", query_low, keys_ext, preferred_element_type=jnp.float32)
        * score_scale
    )
    prob_again = jnp.exp(jnp.where(allowed, scores_again, -1e30) - log_total)
    grad_prob = jnp.einsum("qhd,kd->hqk", grad_att, values_ext, preferred_element_type=jnp.float32)
    inner_sum = jnp.sum(prob_again * grad_prob, axis=-1, keepdims=True)
    grad_scores = (prob_again * (grad_prob - inner_sum)).astype(jnp.bfloat16)
    grad_query = (
        jnp.einsum("hqk,kd->qhd", grad_scores, keys_ext, preferred_element_type=jnp.float32)
        * score_scale
    )
    grad_keys_ext = (
        jnp.einsum("hqk,qhd->kd", grad_scores, query_low, preferred_element_type=jnp.float32)
        * score_scale
    )
    grad_values_ext = jnp.einsum(
        "hqk,qhd->kd", prob_again.astype(jnp.bfloat16), grad_att, preferred_element_type=jnp.float32
    )
    grad_pairs = jnp.concatenate([grad_keys_ext, grad_values_ext], axis=1)
    own_grad = grad_pairs[hop_count * tokens :]
    for distance in range(1, hop_count + 1):
        lower_row = (hop_count - distance) * tokens
        own_grad = own_grad + shifted(grad_pairs[lower_row : lower_row + tokens], "seq", -distance)
    _, back_turn = jax.vjp(turn_norm, query_raw, key_raw, query_gain, key_gain)
    grad_qraw, grad_kraw, grad_qgain, grad_kgain = back_turn((grad_query, own_grad[:, :head_width]))
    grad_raw = jnp.concatenate(
        [
            grad_qraw.astype(jnp.bfloat16),
            grad_kraw.astype(jnp.bfloat16),
            own_grad[:, head_width:].astype(jnp.bfloat16),
        ],
        axis=1,
    )
    into_grad = row_outer(normed, grad_raw)
    grad_normed = back_product(grad_raw, into_w)
    _, back_pre1 = jax.vjp(rms_scale, source, attn_gain)
    grad_source, grad_pre1 = back_pre1(grad_normed)
    grad_input = grad_mid + grad_source
    grads = [
        grad.astype(jnp.bfloat16).reshape(size, -1, grad.shape[-1])
        for grad in (into_grad, output_grad, ffn_grad, down_grad)
    ]
    gain_grads = pack_gains(
        (grad_pre1, grad_post1, grad_pre2, grad_post2, grad_qgain, grad_kgain), 8, (size,)
    )
    piece_widths = [[shards[member].shape[1] for member in group] for group in groups]
    *results, gain_total = reduce_grads(grads, piece_widths, by_rows, shared, gain_grads)
    return (
        result.astype(jnp.bfloat16)[None],
        grad_input.astype(jnp.bfloat16)[None],
        *results,
        *unpack_gains(gain_total[0], widths),
    )


def solution(mesh):
    placed = (
        P("fsdp", "seq", None),
        P("fsdp", "seq", None),
        P("fsdp", None),
        P("fsdp", None),
        P("fsdp", None),
        P("fsdp", None),
        P("fsdp", None),
        P("fsdp", None),
        P("fsdp", None),
        P("fsdp"),
        P("fsdp"),
        P("fsdp"),
        P("fsdp"),
        P("fsdp"),
        P("fsdp"),
    )
    return jax.shard_map(
        on_device,
        mesh=mesh,
        in_specs=placed,
        out_specs=(
            P("fsdp", "seq", None),
            P("fsdp", "seq", None),
            P("fsdp", None),
            P("fsdp", None),
            P("fsdp", None),
            P("fsdp", None),
            P("fsdp", None),
            P("fsdp", None),
            P("fsdp", None),
            P("fsdp"),
            P("fsdp"),
            P("fsdp"),
            P("fsdp"),
            P("fsdp"),
            P("fsdp"),
        ),
        check_vma=False,
    )
```

```python
import functools

import jax
import jax.numpy as jnp
from jax import lax
from jax.experimental import pallas as pl
from jax.experimental.pallas import tpu as pltpu
from jax.sharding import PartitionSpec as P

WINDOW = 512


eps = 1e-06
base_rate = 10000.0


def shifted(array, axis, by):
    size = lax.axis_size(axis)
    pairs = [(i, i + by) for i in range(size) if 0 <= i + by < size]
    return lax.ppermute(array, axis, pairs)


def rms_scale(value, gain):
    return value * lax.rsqrt(jnp.mean(value * value, axis=-1, keepdims=True) + eps) * gain


def rope_tables(positions, head_width):
    half_width = head_width // 2
    frequency = base_rate ** (-jnp.arange(half_width, dtype=jnp.float32) * 2.0 / head_width)
    angles = positions.astype(jnp.float32)[:, None] * frequency[None, :]
    return (jnp.cos(angles), jnp.sin(angles))


def rotate(value, cos_table, sin_table):
    half_width = value.shape[-1] // 2
    first_half = value[..., :half_width]
    second = value[..., half_width:]
    return jnp.concatenate(
        [first_half * cos_table - second * sin_table, second * cos_table + first_half * sin_table],
        axis=-1,
    )


def row_outer(left, right):
    return lax.dot_general(
        left, right, (((0,), (0,)), ((), ())), preferred_element_type=jnp.float32
    )


def back_product(grad_rows, weight):
    return lax.dot_general(
        grad_rows, weight, (((1,), (1,)), ((), ())), preferred_element_type=jnp.float32
    )


MESH = pl.DeviceIdType.MESH
VMEM_BYTES = 56 * 1024 * 1024


def ring_owner(place, size):
    place = lax.rem(place + 2 * size, size)
    return jnp.where(place < size // 2, 2 * place, 2 * (size - 1 - place) + 1)


def ring_place(owner, size):
    return jnp.where(lax.rem(owner, 2) == 0, owner // 2, size - 1 - owner // 2)


def region(shape, by_rows, core, plane=None):
    size = shape[0 if by_rows else 1] // 2
    start = core * size
    if plane is not None:
        size = size // 2
        start = start + plane * size
    if by_rows:
        return (pl.ds(pl.multiple_of(start, size & -size), size), slice(None))
    return (slice(None), pl.ds(pl.multiple_of(start, 128), size))


def region_shape(shape, by_rows, cuts):
    rows, columns = shape
    return (rows // cuts, columns) if by_rows else (rows, columns // cuts)


def greet(peers):
    barrier = pltpu.get_barrier_semaphore()
    for peer in peers:
        pl.semaphore_signal(barrier, inc=1, device_id=peer, device_id_type=MESH)
    pl.semaphore_wait(barrier, len(peers))


def gather_kernel(size, shapes, by_rows, shared, *refs):
    count = len(shapes)
    shards, gains = refs[:count], refs[count]
    refs = refs[count + 1 :]
    wholes, all_gains = refs[:count], refs[count]
    own_sem, ring_send, ring_recv, pair_send, pair_recv = refs[count + 1 : count + 6]
    cross_send, cross_recv, relay_send, relay_recv = refs[count + 6 :]
    seq, me = lax.axis_index("seq"), lax.axis_index("fsdp")
    core, plane = lax.rem(seq, 2), lax.rem(seq // 2, 2)
    way = 1 - 2 * core
    place = ring_place(me, size)
    after = (seq, ring_owner(place + way, size))
    before = (seq, ring_owner(place - way, size))
    pair = (seq + way, me)
    across = (seq + 2 * (1 - 2 * plane), me)

    greet([after, before, pair, across])

    def copy_of(member, block, core, plane, sems, step, device, first=False):
        if member == count:
            target = all_gains.at[block]
            source = gains if first else target
        else:
            part = region(shapes[member], by_rows[member], core, plane)
            target = wholes[member].at[(block, *part)]
            source = shards[member].at[part] if first else target
        return pltpu.make_async_remote_copy(
            src_ref=source,
            dst_ref=target,
            send_sem=sems[0].at[step, member],
            recv_sem=sems[1].at[step, member],
            device_id=device,
            device_id_type=MESH,
        )

    def plane_of(member):
        return plane if member < count and shared[member] else None

    def ring_copy(member, block, step, first=False):
        sems = (ring_send, ring_recv)
        return copy_of(member, block, core, plane_of(member), sems, step, after, first)

    def pair_copy(member, block, step, core):
        return copy_of(member, block, core, plane_of(member), (pair_send, pair_recv), step, pair)

    def cross_copy(member, block, step, plane):
        return copy_of(member, block, core, plane, (cross_send, cross_recv), step, across)

    def relay_copy(member, block, step, core):
        return copy_of(member, block, core, 1 - plane, (relay_send, relay_recv), step, pair)

    for member in range(count + 1):
        ring_copy(member, me, 0, first=True).start()
    own = [
        pltpu.make_async_copy(source, target.at[me], own_sem.at[number])
        for number, (source, target) in enumerate(zip((*shards, gains), (*wholes, all_gains)))
    ]
    for copy in own:
        copy.start()

    def arrive(step, forward):
        block = ring_owner(place - way * step, size)
        for member in range(count + 1):
            ring_copy(member, block, step - 1).wait_recv()
            if forward:
                ring_copy(member, block, step).start()
            if member < count:
                if shared[member]:
                    cross_copy(member, block, step - 1, plane).start()
                pair_copy(member, block, step - 1, core).start()

    def relay(step):
        block = ring_owner(place - way * step, size)
        for member in range(count):
            if shared[member]:
                cross_copy(member, block, step - 1, 1 - plane).wait_recv()
                relay_copy(member, block, step - 1, core).start()

    arrive(1, True)

    def turn(step, _):
        arrive(step, True)
        relay(step - 1)
        return 0

    lax.fori_loop(2, size - 1, turn, 0)
    arrive(size - 1, False)
    relay(size - 2)
    relay(size - 1)

    def finish(step, _):
        block = ring_owner(place + way * (step + 1), size)
        for member in range(count + 1):
            ring_copy(member, me, step).wait_send()
            if member < count:
                pair_copy(member, me, step, core).wait_send()
                pair_copy(member, block, step, 1 - core).wait_recv()
                if shared[member]:
                    cross_copy(member, me, step, plane).wait_send()
                    relay_copy(member, me, step, core).wait_send()
                    relay_copy(member, block, step, 1 - core).wait_recv()
        return 0

    lax.fori_loop(0, size - 1, finish, 0)
    for copy in own:
        copy.wait()


def gather_weights(shards, by_rows, shared, gains):
    size = lax.axis_size("fsdp")
    shapes = [shard.shape for shard in shards]
    count = len(shards)
    any_space = pl.BlockSpec(memory_space=pl.ANY)
    copies = pltpu.SemaphoreType.DMA((size - 1, count + 1))
    return pl.pallas_call(
        functools.partial(gather_kernel, size, shapes, by_rows, shared),
        out_shape=[
            jax.ShapeDtypeStruct((size, *shape), gains.dtype) for shape in (*shapes, gains.shape)
        ],
        in_specs=[any_space] * (len(shards) + 1),
        out_specs=[any_space] * (count + 1),
        scratch_shapes=[pltpu.SemaphoreType.DMA((count + 1,)), *[copies] * 8],
        compiler_params=pltpu.CompilerParams(collective_id=0, has_side_effects=True),
        name="gather_weights",
    )(*shards, gains)


def reduce_kernel(size, blocks, shapes, by_rows, shared, places, *refs):
    count = len(shapes)
    every = list(refs)

    def take(number):
        taken = every[:number]
        del every[:number]
        return taken

    mine, (gain_mine,) = take(count), take(1)
    results, (gain_total,) = take(len(places)), take(1)
    totals, parts, landed, crossed = take(count), take(count), take(count), take(count)
    spread, agreed = take(count), take(count)
    gain_sent, gain_landed, gain_spread = take(3)
    pair_send, pair_recv, ring_send, ring_recv, cross_send, cross_recv = take(6)
    spread_send, spread_recv, gain_send, gain_recv = take(4)
    agree_send, agree_recv, last_send, last_recv = take(4)

    seq, me = lax.axis_index("seq"), lax.axis_index("fsdp")
    core, plane = lax.rem(seq, 2), lax.rem(seq // 2, 2)
    way = 1 - 2 * core
    place = ring_place(me, size)
    after = (seq, ring_owner(place + way, size))
    before = (seq, ring_owner(place - way, size))
    pair = (seq + way, me)
    across = (seq + 2 * (1 - 2 * plane), me)
    others = [(lax.rem(seq + by, blocks), me) for by in range(1, blocks)]
    greet([after, before, *others])

    def remote(source, target, sems, index, device):
        return pltpu.make_async_remote_copy(
            src_ref=source,
            dst_ref=target,
            send_sem=sems[0].at[index],
            recv_sem=sems[1].at[index],
            device_id=device,
            device_id_type=MESH,
        )

    def block_at(step):
        return ring_owner(place - way * (1 + step), size)

    def within(member, part):
        shape = region_shape(shapes[member], by_rows[member], 2)
        return region(shape, by_rows[member], part)

    def ring_part(member):
        return within(member, plane) if shared[member] else (slice(None), slice(None))

    def own_part(member, part):
        return region(shapes[member], by_rows[member], core, part if shared[member] else None)

    def pair_copy(member, step):
        block = ring_owner(place + way * (1 + step), size)
        part = region(shapes[member], by_rows[member], 1 - core)
        return remote(
            mine[member].at[(block, *part)],
            parts[member].at[block],
            (pair_send, pair_recv),
            (step, member),
            pair,
        )

    def ring_copy(member, step):
        if member == count:
            source, target = gain_sent.at[step], gain_landed.at[step]
        else:
            source = parts[member].at[(block_at(step), *ring_part(member))]
            target = landed[member].at[step]
        return remote(source, target, (ring_send, ring_recv), (step, member), after)

    def cross_copy(member, step):
        source = parts[member].at[(block_at(step), *within(member, 1 - plane))]
        return remote(
            source, crossed[member].at[step], (cross_send, cross_recv), (step, member), across
        )

    def start_pair(step, _):
        for member in range(count):
            pair_copy(member, step).start()
        return 0

    lax.fori_loop(0, size, start_pair, 0)

    def prepare(step):
        block = block_at(step)
        for member in range(count):
            pair_copy(member, step).wait_recv()
            if shared[member]:
                spot = (block, *within(member, 1 - plane))
                total = mine[member][(block, *own_part(member, 1 - plane))].astype(jnp.float32)
                total = total + parts[member][spot].astype(jnp.float32)
                parts[member][spot] = total.astype(jnp.bfloat16)
                cross_copy(member, step).start()

    def add_up(step, first, last):
        block = block_at(step)
        for member in range(count):
            spot = (block, *ring_part(member))
            total = mine[member][(block, *own_part(member, plane))].astype(jnp.float32)
            total = total + parts[member][spot].astype(jnp.float32)
            if shared[member]:
                cross_copy(member, step).wait_recv()
                total = total + crossed[member][step].astype(jnp.float32)
            if not first:
                ring_copy(member, step - 1).wait_recv()
                total = total + landed[member][step - 1].astype(jnp.float32)
            if last:
                spread[member][row_of(member)] = total.astype(jnp.bfloat16)
                for by in range(1, rows_of(member)):
                    spread_copy(member, by).start()
            else:
                parts[member][spot] = total.astype(jnp.bfloat16)
                ring_copy(member, step).start()
        total = gain_mine[block]
        if not first:
            ring_copy(count, step - 1).wait_recv()
            total = total + gain_landed[step - 1]
        if last:
            gain_spread[seq] = total
            for by in range(1, blocks):
                gain_copy(by).start()
        else:
            gain_sent[step] = total
            ring_copy(count, step).start()

    def stride_of(member):
        return 4 if shared[member] else 2

    def row_of(member):
        return seq // stride_of(member)

    def rows_of(member):
        return blocks // stride_of(member)

    def spread_copy(member, by):
        target = spread[member].at[row_of(member)]
        device = (lax.rem(seq + stride_of(member) * by, blocks), me)
        return remote(target, target, (spread_send, spread_recv), (by - 1, member), device)

    def gain_copy(by):
        target = gain_spread.at[seq]
        return remote(target, target, (gain_send, gain_recv), by - 1, others[by - 1])

    def agree_copy(member):
        target = agreed[member].at[within(member, plane)]
        return remote(target, target, (agree_send, agree_recv), member, across)

    def last_copy(member):
        target = totals[member].at[region(shapes[member], by_rows[member], core)]
        return remote(target, target, (last_send, last_recv), member, pair)

    prepare(0)
    prepare(1)
    add_up(0, True, False)

    def turn(step, _):
        prepare(step + 1)
        add_up(step, False, False)
        return 0

    lax.fori_loop(1, size - 1, turn, 0)
    add_up(size - 1, False, True)
    order = sorted(range(count), key=lambda member: not shared[member])
    for member in order:
        for by in range(1, rows_of(member)):
            spread_copy(member, by).wait_recv()
        total = spread[member][0].astype(jnp.float32)
        for other in range(1, rows_of(member)):
            total = total + spread[member][other].astype(jnp.float32)
        if shared[member]:
            agreed[member][within(member, plane)] = total.astype(jnp.bfloat16)
            agree_copy(member).start()
        else:
            totals[member][region(shapes[member], by_rows[member], core)] = total
            last_copy(member).start()
    for member in order:
        if shared[member]:
            agree_copy(member).wait_recv()
            total = agreed[member][...].astype(jnp.float32)
            totals[member][region(shapes[member], by_rows[member], core)] = total
            last_copy(member).start()
    for by in range(1, blocks):
        gain_copy(by).wait_recv()
    total = gain_spread[0]
    for other in range(1, blocks):
        total = total + gain_spread[other]
    gain_total[...] = total

    def finish(step, _):
        for member in range(count + 1):
            ring_copy(member, step).wait_send()
        return 0

    lax.fori_loop(0, size - 1, finish, 0)

    def finish_pair(step, _):
        for member in range(count):
            pair_copy(member, step).wait_send()
            if shared[member]:
                cross_copy(member, step).wait_send()
        return 0

    lax.fori_loop(0, size, finish_pair, 0)
    for member in range(count):
        for by in range(1, rows_of(member)):
            spread_copy(member, by).wait_send()
        if shared[member]:
            agree_copy(member).wait_send()
        last_copy(member).wait()
    for by in range(1, blocks):
        gain_copy(by).wait_send()
    for result, (member, column) in zip(results, places):
        result[...] = totals[member][:, column : column + result.shape[1]]


def reduce_grads(grads, widths, by_rows, shared, gain_grads):
    size, blocks = lax.axis_size("fsdp"), lax.axis_size("seq")
    shapes = [grad.shape[1:] for grad in grads]
    count = len(grads)
    halves = [region_shape(shapes[m], by_rows[m], 2) for m in range(count)]
    pieces = [region_shape(shapes[m], by_rows[m], 4 if shared[m] else 2) for m in range(count)]
    places, results = [], []
    for member in range(count):
        column = 0
        for width in widths[member]:
            places.append((member, column))
            results.append((shapes[member][0], width))
            column += width
    gain_shape = gain_grads.shape[1:]
    in_vmem = pl.BlockSpec(memory_space=pltpu.VMEM)
    dma = pltpu.SemaphoreType.DMA
    unused = (16, 128)

    def buffers(lengths, extents):
        return [
            pltpu.VMEM((*length, *extent), jnp.bfloat16)
            for length, extent in zip(lengths, extents)
        ]

    return pl.pallas_call(
        functools.partial(reduce_kernel, size, blocks, shapes, by_rows, shared, places),
        out_shape=[jax.ShapeDtypeStruct(shape, jnp.float32) for shape in (*results, gain_shape)],
        in_specs=[in_vmem] * (count + 1),
        out_specs=[in_vmem] * (len(results) + 1),
        scratch_shapes=[
            *[pltpu.VMEM(shape, jnp.float32) for shape in shapes],
            *buffers([(size,)] * count, halves),
            *buffers([(size - 1,)] * count, pieces),
            *buffers(
                [(size,) if member else () for member in shared],
                [pieces[m] if shared[m] else unused for m in range(count)],
            ),
            *buffers([(blocks // (4 if member else 2),) for member in shared], pieces),
            *buffers([()] * count, [halves[m] if shared[m] else unused for m in range(count)]),
            pltpu.VMEM((size - 1, *gain_shape), jnp.float32),
            pltpu.VMEM((size - 1, *gain_shape), jnp.float32),
            pltpu.VMEM((blocks, *gain_shape), jnp.float32),
            dma((size, count)),
            dma((size, count)),
            dma((size - 1, count + 1)),
            dma((size - 1, count + 1)),
            dma((size, count)),
            dma((size, count)),
            dma((blocks // 2, count)),
            dma((blocks // 2, count)),
            dma((blocks,)),
            dma((blocks,)),
            dma((count,)),
            dma((count,)),
            dma((count,)),
            dma((count,)),
        ],
        compiler_params=pltpu.CompilerParams(
            collective_id=1, has_side_effects=True, vmem_limit_bytes=VMEM_BYTES
        ),
        name="reduce_grads",
    )(*grads, gain_grads)


def pack_gains(members, rows):
    columns = -(-max(member.shape[-1] for member in members) // 128) * 128
    padded = [
        jnp.pad(member, [(0, 0)] * (member.ndim - 1) + [(0, columns - member.shape[-1])])
        for member in members
    ]
    padded += [jnp.zeros_like(padded[0])] * (rows - len(members))
    return jnp.stack(padded, axis=-2)


def unpack_gains(rows, widths):
    return [rows[..., place, :width] for place, width in enumerate(widths)]


def on_device(
    inputs,
    cotangent,
    query_proj,
    key_proj,
    value_proj,
    output_proj,
    gate_proj,
    up_proj,
    down_proj,
    attn_norm,
    attn_post_norm,
    ffn_norm,
    ffn_post_norm,
    query_norm,
    key_norm,
):
    size = lax.axis_size("fsdp")
    shards = (query_proj, key_proj, value_proj, output_proj, gate_proj, up_proj, down_proj)
    groups = ((0, 1, 2), (3,), (4, 5), (6,))
    by_rows = (False, True, False, True)
    shared = (False, True, True, False)
    gain_shards = (attn_norm, attn_post_norm, ffn_norm, ffn_post_norm, query_norm, key_norm)
    widths = [member.shape[0] for member in gain_shards]
    *wholes, all_gains = gather_weights(
        [jnp.concatenate([shards[member] for member in group], axis=1) for group in groups],
        by_rows,
        shared,
        pack_gains(gain_shards, 16),
    )
    into_w, output_w, ffn_w, down_w = (whole.reshape(-1, whole.shape[-1]) for whole in wholes)
    query_width, head_width = query_proj.shape[1], key_proj.shape[1]
    ffn_width = gate_proj.shape[1]
    attn_gain, attn_post_gain, ffn_gain, ffn_post_gain, query_gain, key_gain = (
        piece.reshape(-1).astype(jnp.float32) for piece in unpack_gains(all_gains, widths)
    )
    source = inputs[0].astype(jnp.float32)
    tokens = source.shape[0]
    head_count = query_width // head_width
    score_scale = head_width ** (-0.5)
    hop_count = min((WINDOW + tokens - 2) // tokens, lax.axis_size("seq") - 1)
    seq_place = lax.axis_index("seq")
    positions = seq_place * tokens + jnp.arange(tokens, dtype=jnp.int32)
    cos_table, sin_table = rope_tables(positions, head_width)
    normed = rms_scale(source, attn_gain).astype(jnp.bfloat16)
    raw = jnp.dot(normed, into_w, preferred_element_type=jnp.float32)
    query_raw = raw[:, :query_width]
    key_raw = raw[:, query_width : query_width + head_width]
    value_raw = raw[:, query_width + head_width :]

    def turn_norm(query_in, key_in, q_gain, k_gain):
        query_out = rotate(
            rms_scale(query_in.reshape(tokens, head_count, head_width), q_gain),
            cos_table[:, None, :],
            sin_table[:, None, :],
        )
        key_out = rotate(rms_scale(key_in, k_gain), cos_table, sin_table)
        return (query_out, key_out)

    query_rot, key_rot = turn_norm(query_raw, key_raw, query_gain, key_gain)
    query_low = query_rot.astype(jnp.bfloat16)
    own_pairs = jnp.concatenate(
        [key_rot.astype(jnp.bfloat16), value_raw.astype(jnp.bfloat16)], axis=1
    )
    received = []
    for distance in range(1, hop_count + 1):
        received.append(shifted(own_pairs, "seq", distance))
    key_value = jnp.concatenate(received[::-1] + [own_pairs], axis=0)
    keys_ext = key_value[:, :head_width]
    values_ext = key_value[:, head_width:]
    ext_rows = key_value.shape[0]
    key_pos = (seq_place - hop_count) * tokens + jnp.arange(ext_rows, dtype=jnp.int32)
    offset = positions[:, None] - key_pos[None, :]
    allowed = ((offset >= 0) & (offset < WINDOW) & (key_pos[None, :] >= 0))[None]
    scores = (
        jnp.einsum("qhd,kd->hqk", query_low, keys_ext, preferred_element_type=jnp.float32)
        * score_scale
    )
    masked = jnp.where(allowed, scores, -1e30)
    row_max = jnp.max(masked, axis=-1, keepdims=True)
    raised = jnp.exp(masked - row_max)
    row_sum = jnp.sum(raised, axis=-1, keepdims=True)
    attn_prob = raised / row_sum
    log_total = row_max + jnp.log(row_sum)
    attended = jnp.einsum(
        "hqk,kd->qhd",
        attn_prob.astype(jnp.bfloat16),
        values_ext,
        preferred_element_type=jnp.float32,
    )
    att_low = attended.reshape(tokens, head_count * head_width).astype(jnp.bfloat16)
    branch = jnp.dot(att_low, output_w, preferred_element_type=jnp.float32)
    middle = source + rms_scale(branch, attn_post_gain)
    normed2 = rms_scale(middle, ffn_gain).astype(jnp.bfloat16)
    both = jnp.dot(normed2, ffn_w, preferred_element_type=jnp.float32)
    gate_val, upper = both[:, :ffn_width], both[:, ffn_width:]

    def act_piece(gate_in, upper_in):
        return jax.nn.gelu(gate_in, approximate=True) * upper_in

    hidden = act_piece(gate_val, upper).astype(jnp.bfloat16)
    down_out = jnp.dot(hidden, down_w, preferred_element_type=jnp.float32)
    result = middle + rms_scale(down_out, ffn_post_gain)
    grad_y = cotangent[0].astype(jnp.float32)
    _, back_post2 = jax.vjp(rms_scale, down_out, ffn_post_gain)
    grad_down, grad_post2 = back_post2(grad_y)
    grad_down_low = grad_down.astype(jnp.bfloat16)
    down_grad = row_outer(hidden, grad_down_low)
    grad_hidden = back_product(grad_down_low, down_w)
    _, back_act = jax.vjp(act_piece, gate_val, upper)
    grad_gate, grad_up = back_act(grad_hidden)
    grad_both = jnp.concatenate(
        [grad_gate.astype(jnp.bfloat16), grad_up.astype(jnp.bfloat16)], axis=1
    )
    ffn_grad = row_outer(normed2, grad_both)
    grad_normed2 = back_product(grad_both, ffn_w)
    _, back_pre2 = jax.vjp(rms_scale, middle, ffn_gain)
    grad_mid_norm, grad_pre2 = back_pre2(grad_normed2)
    grad_mid = grad_y + grad_mid_norm
    _, back_post1 = jax.vjp(rms_scale, branch, attn_post_gain)
    grad_branch, grad_post1 = back_post1(grad_mid)
    grad_branch_low = grad_branch.astype(jnp.bfloat16)
    output_grad = row_outer(att_low, grad_branch_low)
    grad_att = (
        back_product(grad_branch_low, output_w)
        .astype(jnp.bfloat16)
        .reshape(tokens, head_count, head_width)
    )
    scores_again = (
        jnp.einsum("qhd,kd->hqk", query_low, keys_ext, preferred_element_type=jnp.float32)
        * score_scale
    )
    prob_again = jnp.exp(jnp.where(allowed, scores_again, -1e30) - log_total)
    grad_prob = jnp.einsum("qhd,kd->hqk", grad_att, values_ext, preferred_element_type=jnp.float32)
    inner_sum = jnp.sum(prob_again * grad_prob, axis=-1, keepdims=True)
    grad_scores = (prob_again * (grad_prob - inner_sum)).astype(jnp.bfloat16)
    grad_query = (
        jnp.einsum("hqk,kd->qhd", grad_scores, keys_ext, preferred_element_type=jnp.float32)
        * score_scale
    )
    grad_keys_ext = (
        jnp.einsum("hqk,qhd->kd", grad_scores, query_low, preferred_element_type=jnp.float32)
        * score_scale
    )
    grad_values_ext = jnp.einsum(
        "hqk,qhd->kd", prob_again.astype(jnp.bfloat16), grad_att, preferred_element_type=jnp.float32
    )
    grad_pairs = jnp.concatenate([grad_keys_ext, grad_values_ext], axis=1)
    own_grad = grad_pairs[hop_count * tokens :]
    for distance in range(1, hop_count + 1):
        lower_row = (hop_count - distance) * tokens
        own_grad = own_grad + shifted(grad_pairs[lower_row : lower_row + tokens], "seq", -distance)
    _, back_turn = jax.vjp(turn_norm, query_raw, key_raw, query_gain, key_gain)
    grad_qraw, grad_kraw, grad_qgain, grad_kgain = back_turn((grad_query, own_grad[:, :head_width]))
    grad_raw = jnp.concatenate(
        [
            grad_qraw.astype(jnp.bfloat16),
            grad_kraw.astype(jnp.bfloat16),
            own_grad[:, head_width:].astype(jnp.bfloat16),
        ],
        axis=1,
    )
    into_grad = row_outer(normed, grad_raw)
    grad_normed = back_product(grad_raw, into_w)
    _, back_pre1 = jax.vjp(rms_scale, source, attn_gain)
    grad_source, grad_pre1 = back_pre1(grad_normed)
    grad_input = grad_mid + grad_source
    grads = [
        grad.astype(jnp.bfloat16).reshape(size, -1, grad.shape[-1])
        for grad in (into_grad, output_grad, ffn_grad, down_grad)
    ]
    local = (grad_pre1, grad_post1, grad_pre2, grad_post2, grad_qgain, grad_kgain)
    gain_grads = pack_gains([member.reshape(size, -1) for member in local], 8)
    piece_widths = [[shards[member].shape[1] for member in group] for group in groups]
    *results, gain_total = reduce_grads(grads, piece_widths, by_rows, shared, gain_grads)
    return (
        result.astype(jnp.bfloat16)[None],
        grad_input.astype(jnp.bfloat16)[None],
        *results,
        *unpack_gains(gain_total, widths),
    )


def solution(mesh):
    placed = (
        P("fsdp", "seq", None),
        P("fsdp", "seq", None),
        P("fsdp", None),
        P("fsdp", None),
        P("fsdp", None),
        P("fsdp", None),
        P("fsdp", None),
        P("fsdp", None),
        P("fsdp", None),
        P("fsdp"),
        P("fsdp"),
        P("fsdp"),
        P("fsdp"),
        P("fsdp"),
        P("fsdp"),
    )
    return jax.shard_map(
        on_device,
        mesh=mesh,
        in_specs=placed,
        out_specs=(
            P("fsdp", "seq", None),
            P("fsdp", "seq", None),
            P("fsdp", None),
            P("fsdp", None),
            P("fsdp", None),
            P("fsdp", None),
            P("fsdp", None),
            P("fsdp", None),
            P("fsdp", None),
            P("fsdp"),
            P("fsdp"),
            P("fsdp"),
            P("fsdp"),
            P("fsdp"),
            P("fsdp"),
        ),
        check_vma=False,
    )
```

```python
import functools

import jax
import jax.numpy as jnp
from jax import lax
from jax.experimental import pallas as pl
from jax.experimental.pallas import tpu as pltpu
from jax.sharding import PartitionSpec as P

WINDOW = 512


eps = 1e-06
base_rate = 10000.0


def shifted(array, axis, by):
    size = lax.axis_size(axis)
    pairs = [(i, i + by) for i in range(size) if 0 <= i + by < size]
    return lax.ppermute(array, axis, pairs)


def rms_scale(value, gain):
    return value * lax.rsqrt(jnp.mean(value * value, axis=-1, keepdims=True) + eps) * gain


def rope_tables(positions, head_width):
    half_width = head_width // 2
    frequency = base_rate ** (-jnp.arange(half_width, dtype=jnp.float32) * 2.0 / head_width)
    angles = positions.astype(jnp.float32)[:, None] * frequency[None, :]
    return (jnp.cos(angles), jnp.sin(angles))


def rotate(value, cos_table, sin_table):
    half_width = value.shape[-1] // 2
    first_half = value[..., :half_width]
    second = value[..., half_width:]
    return jnp.concatenate(
        [first_half * cos_table - second * sin_table, second * cos_table + first_half * sin_table],
        axis=-1,
    )


def row_outer(left, right):
    return lax.dot_general(
        left, right, (((0,), (0,)), ((), ())), preferred_element_type=jnp.float32
    )


def back_product(grad_rows, weight):
    return lax.dot_general(
        grad_rows, weight, (((1,), (1,)), ((), ())), preferred_element_type=jnp.float32
    )


MESH = pl.DeviceIdType.MESH
VMEM_BYTES = 56 * 1024 * 1024


def ring_owner(place, size):
    place = lax.rem(place + 2 * size, size)
    return jnp.where(place < size // 2, 2 * place, 2 * (size - 1 - place) + 1)


def ring_place(owner, size):
    return jnp.where(lax.rem(owner, 2) == 0, owner // 2, size - 1 - owner // 2)


def region(shape, by_rows, core, plane=None):
    size = shape[0 if by_rows else 1] // 2
    start = core * size
    if plane is not None:
        size = size // 2
        start = start + plane * size
    if by_rows:
        return (pl.ds(pl.multiple_of(start, size & -size), size), slice(None))
    return (slice(None), pl.ds(pl.multiple_of(start, 128), size))


def region_shape(shape, by_rows, cuts):
    rows, columns = shape
    return (rows // cuts, columns) if by_rows else (rows, columns // cuts)


def greet(peers):
    barrier = pltpu.get_barrier_semaphore()
    for peer in peers:
        pl.semaphore_signal(barrier, inc=1, device_id=peer, device_id_type=MESH)
    pl.semaphore_wait(barrier, len(peers))


def gather_kernel(size, shapes, by_rows, shared, *refs):
    count = len(shapes)
    shards, gains = refs[:count], refs[count]
    refs = refs[count + 1 :]
    wholes, all_gains = refs[:count], refs[count]
    own_sem, ring_send, ring_recv, pair_send, pair_recv = refs[count + 1 : count + 6]
    cross_send, cross_recv, relay_send, relay_recv = refs[count + 6 :]
    seq, me = lax.axis_index("seq"), lax.axis_index("fsdp")
    core, plane = lax.rem(seq, 2), lax.rem(seq // 2, 2)
    way = 1 - 2 * core
    place = ring_place(me, size)
    after = (seq, ring_owner(place + way, size))
    before = (seq, ring_owner(place - way, size))
    pair = (seq + way, me)
    across = (seq + 2 * (1 - 2 * plane), me)

    greet([after, before, pair, across])

    def copy_of(member, block, core, plane, sems, step, device, first=False):
        if member == count:
            target = all_gains.at[block]
            source = gains if first else target
        else:
            part = region(shapes[member], by_rows[member], core, plane)
            target = wholes[member].at[(block, *part)]
            source = shards[member].at[part] if first else target
        return pltpu.make_async_remote_copy(
            src_ref=source,
            dst_ref=target,
            send_sem=sems[0].at[step, member],
            recv_sem=sems[1].at[step, member],
            device_id=device,
            device_id_type=MESH,
        )

    def plane_of(member):
        return plane if member < count and shared[member] else None

    def ring_copy(member, block, step, first=False):
        sems = (ring_send, ring_recv)
        return copy_of(member, block, core, plane_of(member), sems, step, after, first)

    def pair_copy(member, block, step, core):
        return copy_of(member, block, core, plane_of(member), (pair_send, pair_recv), step, pair)

    def cross_copy(member, block, step, plane):
        return copy_of(member, block, core, plane, (cross_send, cross_recv), step, across)

    def relay_copy(member, block, step, core):
        return copy_of(member, block, core, 1 - plane, (relay_send, relay_recv), step, pair)

    for member in range(count + 1):
        ring_copy(member, me, 0, first=True).start()
    own = [
        pltpu.make_async_copy(source, target.at[me], own_sem.at[number])
        for number, (source, target) in enumerate(zip((*shards, gains), (*wholes, all_gains)))
    ]
    for copy in own:
        copy.start()

    def arrive(step, forward):
        block = ring_owner(place - way * step, size)
        for member in range(count + 1):
            ring_copy(member, block, step - 1).wait_recv()
            if forward:
                ring_copy(member, block, step).start()
            if member < count:
                if shared[member]:
                    cross_copy(member, block, step - 1, plane).start()
                pair_copy(member, block, step - 1, core).start()

    def relay(step):
        block = ring_owner(place - way * step, size)
        for member in range(count):
            if shared[member]:
                cross_copy(member, block, step - 1, 1 - plane).wait_recv()
                relay_copy(member, block, step - 1, core).start()

    arrive(1, True)

    def turn(step, _):
        arrive(step, True)
        relay(step - 1)
        return 0

    lax.fori_loop(2, size - 1, turn, 0)
    arrive(size - 1, False)
    relay(size - 2)
    relay(size - 1)

    def finish(step, _):
        block = ring_owner(place + way * (step + 1), size)
        for member in range(count + 1):
            ring_copy(member, me, step).wait_send()
            if member < count:
                pair_copy(member, me, step, core).wait_send()
                pair_copy(member, block, step, 1 - core).wait_recv()
                if shared[member]:
                    cross_copy(member, me, step, plane).wait_send()
                    relay_copy(member, me, step, core).wait_send()
                    relay_copy(member, block, step, 1 - core).wait_recv()
        return 0

    lax.fori_loop(0, size - 1, finish, 0)
    for copy in own:
        copy.wait()


def gather_weights(shards, by_rows, shared, gains):
    size = lax.axis_size("fsdp")
    shapes = [shard.shape for shard in shards]
    count = len(shards)
    any_space = pl.BlockSpec(memory_space=pl.ANY)
    copies = pltpu.SemaphoreType.DMA((size - 1, count + 1))
    return pl.pallas_call(
        functools.partial(gather_kernel, size, shapes, by_rows, shared),
        out_shape=[
            jax.ShapeDtypeStruct((size, *shape), gains.dtype) for shape in (*shapes, gains.shape)
        ],
        in_specs=[any_space] * (len(shards) + 1),
        out_specs=[any_space] * (count + 1),
        scratch_shapes=[pltpu.SemaphoreType.DMA((count + 1,)), *[copies] * 8],
        compiler_params=pltpu.CompilerParams(collective_id=0, has_side_effects=True),
        name="gather_weights",
    )(*shards, gains)


def reduce_kernel(size, blocks, shapes, by_rows, shared, places, *refs):
    count = len(shapes)
    every = list(refs)

    def take(number):
        taken = every[:number]
        del every[:number]
        return taken

    grads, (gain_mine,) = take(count), take(1)
    results, (gain_total,) = take(len(places)), take(1)
    totals, mine, parts = take(count), take(count), take(count)
    landed, crossed = take(count), take(count)
    spread, agreed = take(count), take(count)
    gain_sent, gain_landed, gain_spread = take(3)
    pair_send, pair_recv, ring_send, ring_recv, cross_send, cross_recv = take(6)
    spread_send, spread_recv, gain_send, gain_recv = take(4)
    agree_send, agree_recv, last_send, last_recv, own_sem = take(5)

    seq, me = lax.axis_index("seq"), lax.axis_index("fsdp")
    core, plane = lax.rem(seq, 2), lax.rem(seq // 2, 2)
    way = 1 - 2 * core
    place = ring_place(me, size)
    after = (seq, ring_owner(place + way, size))
    before = (seq, ring_owner(place - way, size))
    pair = (seq + way, me)
    across = (seq + 2 * (1 - 2 * plane), me)
    others = [(lax.rem(seq + by, blocks), me) for by in range(1, blocks)]
    greet([after, before, *others])

    def remote(source, target, sems, index, device):
        return pltpu.make_async_remote_copy(
            src_ref=source,
            dst_ref=target,
            send_sem=sems[0].at[index],
            recv_sem=sems[1].at[index],
            device_id=device,
            device_id_type=MESH,
        )

    def block_at(step):
        return ring_owner(place - way * (1 + step), size)

    def within(member, part):
        shape = region_shape(shapes[member], by_rows[member], 2)
        return region(shape, by_rows[member], part)

    def ring_part(member):
        return within(member, plane) if shared[member] else (slice(None), slice(None))

    def own_copy(member, step):
        part = region(shapes[member], by_rows[member], core)
        source = grads[member].at[(block_at(step), *part)]
        return pltpu.make_async_copy(
            source, mine[member].at[block_at(step)], own_sem.at[step, member]
        )

    def pair_copy(member, step):
        block = ring_owner(place + way * (1 + step), size)
        part = region(shapes[member], by_rows[member], 1 - core)
        return remote(
            grads[member].at[(block, *part)],
            parts[member].at[block],
            (pair_send, pair_recv),
            (step, member),
            pair,
        )

    def ring_copy(member, step):
        if member == count:
            source, target = gain_sent.at[step], gain_landed.at[step]
        else:
            source = parts[member].at[(block_at(step), *ring_part(member))]
            target = landed[member].at[step]
        return remote(source, target, (ring_send, ring_recv), (step, member), after)

    def cross_copy(member, step):
        source = parts[member].at[(block_at(step), *within(member, 1 - plane))]
        return remote(
            source, crossed[member].at[step], (cross_send, cross_recv), (step, member), across
        )

    def start_pair(step, _):
        for member in range(count):
            own_copy(member, step).start()
            pair_copy(member, step).start()
        return 0

    lax.fori_loop(0, size, start_pair, 0)

    def prepare(step):
        block = block_at(step)
        for member in range(count):
            own_copy(member, step).wait()
            pair_copy(member, step).wait_recv()
            if shared[member]:
                spot = (block, *within(member, 1 - plane))
                total = mine[member][spot].astype(jnp.float32)
                total = total + parts[member][spot].astype(jnp.float32)
                parts[member][spot] = total.astype(jnp.bfloat16)
                cross_copy(member, step).start()

    def add_up(step, first, last):
        block = block_at(step)
        for member in range(count):
            spot = (block, *ring_part(member))
            total = mine[member][spot].astype(jnp.float32)
            total = total + parts[member][spot].astype(jnp.float32)
            if shared[member]:
                cross_copy(member, step).wait_recv()
                total = total + crossed[member][step].astype(jnp.float32)
            if not first:
                ring_copy(member, step - 1).wait_recv()
                total = total + landed[member][step - 1].astype(jnp.float32)
            if last:
                spread[member][row_of(member)] = total.astype(jnp.bfloat16)
                for by in range(1, rows_of(member)):
                    spread_copy(member, by).start()
            else:
                parts[member][spot] = total.astype(jnp.bfloat16)
                ring_copy(member, step).start()
        total = gain_mine[block]
        if not first:
            ring_copy(count, step - 1).wait_recv()
            total = total + gain_landed[step - 1]
        if last:
            gain_spread[seq] = total
            for by in range(1, blocks):
                gain_copy(by).start()
        else:
            gain_sent[step] = total
            ring_copy(count, step).start()

    def stride_of(member):
        return 4 if shared[member] else 2

    def row_of(member):
        return seq // stride_of(member)

    def rows_of(member):
        return blocks // stride_of(member)

    def spread_copy(member, by):
        target = spread[member].at[row_of(member)]
        device = (lax.rem(seq + stride_of(member) * by, blocks), me)
        return remote(target, target, (spread_send, spread_recv), (by - 1, member), device)

    def gain_copy(by):
        target = gain_spread.at[seq]
        return remote(target, target, (gain_send, gain_recv), by - 1, others[by - 1])

    def agree_copy(member):
        target = agreed[member].at[within(member, plane)]
        return remote(target, target, (agree_send, agree_recv), member, across)

    def last_copy(member):
        target = totals[member].at[region(shapes[member], by_rows[member], core)]
        return remote(target, target, (last_send, last_recv), member, pair)

    prepare(0)
    prepare(1)
    add_up(0, True, False)

    def turn(step, _):
        prepare(step + 1)
        add_up(step, False, False)
        return 0

    lax.fori_loop(1, size - 1, turn, 0)
    add_up(size - 1, False, True)
    order = sorted(range(count), key=lambda member: not shared[member])
    for member in order:
        for by in range(1, rows_of(member)):
            spread_copy(member, by).wait_recv()
        total = spread[member][0].astype(jnp.float32)
        for other in range(1, rows_of(member)):
            total = total + spread[member][other].astype(jnp.float32)
        if shared[member]:
            agreed[member][within(member, plane)] = total.astype(jnp.bfloat16)
            agree_copy(member).start()
        else:
            totals[member][region(shapes[member], by_rows[member], core)] = total
            last_copy(member).start()
    for member in order:
        if shared[member]:
            agree_copy(member).wait_recv()
            total = agreed[member][...].astype(jnp.float32)
            totals[member][region(shapes[member], by_rows[member], core)] = total
            last_copy(member).start()
    for by in range(1, blocks):
        gain_copy(by).wait_recv()
    total = gain_spread[0]
    for other in range(1, blocks):
        total = total + gain_spread[other]
    gain_total[...] = total

    def finish(step, _):
        for member in range(count + 1):
            ring_copy(member, step).wait_send()
        return 0

    lax.fori_loop(0, size - 1, finish, 0)

    def finish_pair(step, _):
        for member in range(count):
            pair_copy(member, step).wait_send()
            if shared[member]:
                cross_copy(member, step).wait_send()
        return 0

    lax.fori_loop(0, size, finish_pair, 0)
    for member in range(count):
        for by in range(1, rows_of(member)):
            spread_copy(member, by).wait_send()
        if shared[member]:
            agree_copy(member).wait_send()
        last_copy(member).wait()
    for by in range(1, blocks):
        gain_copy(by).wait_send()
    for result, (member, column) in zip(results, places):
        result[...] = totals[member][:, column : column + result.shape[1]]


def reduce_grads(grads, widths, by_rows, shared, gain_grads):
    size, blocks = lax.axis_size("fsdp"), lax.axis_size("seq")
    shapes = [grad.shape[1:] for grad in grads]
    count = len(grads)
    halves = [region_shape(shapes[m], by_rows[m], 2) for m in range(count)]
    pieces = [region_shape(shapes[m], by_rows[m], 4 if shared[m] else 2) for m in range(count)]
    places, results = [], []
    for member in range(count):
        column = 0
        for width in widths[member]:
            places.append((member, column))
            results.append((shapes[member][0], width))
            column += width
    gain_shape = gain_grads.shape[1:]
    in_vmem = pl.BlockSpec(memory_space=pltpu.VMEM)
    dma = pltpu.SemaphoreType.DMA
    unused = (16, 128)

    def buffers(lengths, extents):
        return [
            pltpu.VMEM((*length, *extent), jnp.bfloat16)
            for length, extent in zip(lengths, extents)
        ]

    return pl.pallas_call(
        functools.partial(reduce_kernel, size, blocks, shapes, by_rows, shared, places),
        out_shape=[jax.ShapeDtypeStruct(shape, jnp.float32) for shape in (*results, gain_shape)],
        in_specs=[pl.BlockSpec(memory_space=pl.ANY)] * count + [in_vmem],
        out_specs=[in_vmem] * (len(results) + 1),
        scratch_shapes=[
            *[pltpu.VMEM(shape, jnp.float32) for shape in shapes],
            *buffers([(size,)] * count, halves),
            *buffers([(size,)] * count, halves),
            *buffers([(size - 1,)] * count, pieces),
            *buffers(
                [(size,) if member else () for member in shared],
                [pieces[m] if shared[m] else unused for m in range(count)],
            ),
            *buffers([(blocks // (4 if member else 2),) for member in shared], pieces),
            *buffers([()] * count, [halves[m] if shared[m] else unused for m in range(count)]),
            pltpu.VMEM((size - 1, *gain_shape), jnp.float32),
            pltpu.VMEM((size - 1, *gain_shape), jnp.float32),
            pltpu.VMEM((blocks, *gain_shape), jnp.float32),
            dma((size, count)),
            dma((size, count)),
            dma((size - 1, count + 1)),
            dma((size - 1, count + 1)),
            dma((size, count)),
            dma((size, count)),
            dma((blocks // 2, count)),
            dma((blocks // 2, count)),
            dma((blocks,)),
            dma((blocks,)),
            dma((count,)),
            dma((count,)),
            dma((count,)),
            dma((count,)),
            dma((size, count)),
        ],
        compiler_params=pltpu.CompilerParams(
            collective_id=1, has_side_effects=True, vmem_limit_bytes=VMEM_BYTES
        ),
        name="reduce_grads",
    )(*grads, gain_grads)


def pack_gains(members, rows):
    columns = -(-max(member.shape[-1] for member in members) // 128) * 128
    padded = [
        jnp.pad(member, [(0, 0)] * (member.ndim - 1) + [(0, columns - member.shape[-1])])
        for member in members
    ]
    padded += [jnp.zeros_like(padded[0])] * (rows - len(members))
    return jnp.stack(padded, axis=-2)


def unpack_gains(rows, widths):
    return [rows[..., place, :width] for place, width in enumerate(widths)]


def on_device(
    inputs,
    cotangent,
    query_proj,
    key_proj,
    value_proj,
    output_proj,
    gate_proj,
    up_proj,
    down_proj,
    attn_norm,
    attn_post_norm,
    ffn_norm,
    ffn_post_norm,
    query_norm,
    key_norm,
):
    size = lax.axis_size("fsdp")
    shards = (query_proj, key_proj, value_proj, output_proj, gate_proj, up_proj, down_proj)
    groups = ((0, 1, 2), (3,), (4, 5), (6,))
    by_rows = (False, True, False, True)
    shared = (True, False, True, False)
    gain_shards = (attn_norm, attn_post_norm, ffn_norm, ffn_post_norm, query_norm, key_norm)
    widths = [member.shape[0] for member in gain_shards]
    *wholes, all_gains = gather_weights(
        [jnp.concatenate([shards[member] for member in group], axis=1) for group in groups],
        by_rows,
        shared,
        pack_gains(gain_shards, 16),
    )
    into_w, output_w, ffn_w, down_w = (whole.reshape(-1, whole.shape[-1]) for whole in wholes)
    query_width, head_width = query_proj.shape[1], key_proj.shape[1]
    ffn_width = gate_proj.shape[1]
    attn_gain, attn_post_gain, ffn_gain, ffn_post_gain, query_gain, key_gain = (
        piece.reshape(-1).astype(jnp.float32) for piece in unpack_gains(all_gains, widths)
    )
    source = inputs[0].astype(jnp.float32)
    tokens = source.shape[0]
    head_count = query_width // head_width
    score_scale = head_width ** (-0.5)
    hop_count = min((WINDOW + tokens - 2) // tokens, lax.axis_size("seq") - 1)
    seq_place = lax.axis_index("seq")
    positions = seq_place * tokens + jnp.arange(tokens, dtype=jnp.int32)
    cos_table, sin_table = rope_tables(positions, head_width)
    normed = rms_scale(source, attn_gain).astype(jnp.bfloat16)
    raw = jnp.dot(normed, into_w, preferred_element_type=jnp.float32)
    query_raw = raw[:, :query_width]
    key_raw = raw[:, query_width : query_width + head_width]
    value_raw = raw[:, query_width + head_width :]

    def turn_norm(query_in, key_in, q_gain, k_gain):
        query_out = rotate(
            rms_scale(query_in.reshape(tokens, head_count, head_width), q_gain),
            cos_table[:, None, :],
            sin_table[:, None, :],
        )
        key_out = rotate(rms_scale(key_in, k_gain), cos_table, sin_table)
        return (query_out, key_out)

    query_rot, key_rot = turn_norm(query_raw, key_raw, query_gain, key_gain)
    query_low = query_rot.astype(jnp.bfloat16)
    own_pairs = jnp.concatenate(
        [key_rot.astype(jnp.bfloat16), value_raw.astype(jnp.bfloat16)], axis=1
    )
    received = []
    for distance in range(1, hop_count + 1):
        received.append(shifted(own_pairs, "seq", distance))
    key_value = jnp.concatenate(received[::-1] + [own_pairs], axis=0)
    keys_ext = key_value[:, :head_width]
    values_ext = key_value[:, head_width:]
    ext_rows = key_value.shape[0]
    key_pos = (seq_place - hop_count) * tokens + jnp.arange(ext_rows, dtype=jnp.int32)
    offset = positions[:, None] - key_pos[None, :]
    allowed = ((offset >= 0) & (offset < WINDOW) & (key_pos[None, :] >= 0))[None]
    scores = (
        jnp.einsum("qhd,kd->hqk", query_low, keys_ext, preferred_element_type=jnp.float32)
        * score_scale
    )
    masked = jnp.where(allowed, scores, -1e30)
    row_max = jnp.max(masked, axis=-1, keepdims=True)
    raised = jnp.exp(masked - row_max)
    row_sum = jnp.sum(raised, axis=-1, keepdims=True)
    attn_prob = raised / row_sum
    attended = jnp.einsum(
        "hqk,kd->qhd",
        attn_prob.astype(jnp.bfloat16),
        values_ext,
        preferred_element_type=jnp.float32,
    )
    att_low = attended.reshape(tokens, head_count * head_width).astype(jnp.bfloat16)
    branch = jnp.dot(att_low, output_w, preferred_element_type=jnp.float32)
    middle = source + rms_scale(branch, attn_post_gain)
    normed2 = rms_scale(middle, ffn_gain).astype(jnp.bfloat16)
    both = jnp.dot(normed2, ffn_w, preferred_element_type=jnp.float32)
    gate_val, upper = both[:, :ffn_width], both[:, ffn_width:]

    def act_piece(gate_in, upper_in):
        return jax.nn.gelu(gate_in, approximate=True) * upper_in

    hidden = act_piece(gate_val, upper).astype(jnp.bfloat16)
    down_out = jnp.dot(hidden, down_w, preferred_element_type=jnp.float32)
    result = middle + rms_scale(down_out, ffn_post_gain)
    grad_y = cotangent[0].astype(jnp.float32)
    _, back_post2 = jax.vjp(rms_scale, down_out, ffn_post_gain)
    grad_down, grad_post2 = back_post2(grad_y)
    grad_down_low = grad_down.astype(jnp.bfloat16)
    down_grad = row_outer(hidden, grad_down_low)
    grad_hidden = back_product(grad_down_low, down_w)
    _, back_act = jax.vjp(act_piece, gate_val, upper)
    grad_gate, grad_up = back_act(grad_hidden)
    grad_both = jnp.concatenate(
        [grad_gate.astype(jnp.bfloat16), grad_up.astype(jnp.bfloat16)], axis=1
    )
    ffn_grad = row_outer(normed2, grad_both)
    grad_normed2 = back_product(grad_both, ffn_w)
    _, back_pre2 = jax.vjp(rms_scale, middle, ffn_gain)
    grad_mid_norm, grad_pre2 = back_pre2(grad_normed2)
    grad_mid = grad_y + grad_mid_norm
    _, back_post1 = jax.vjp(rms_scale, branch, attn_post_gain)
    grad_branch, grad_post1 = back_post1(grad_mid)
    grad_branch_low = grad_branch.astype(jnp.bfloat16)
    output_grad = row_outer(att_low, grad_branch_low)
    grad_att = (
        back_product(grad_branch_low, output_w)
        .astype(jnp.bfloat16)
        .reshape(tokens, head_count, head_width)
    )
    grad_prob = jnp.einsum("qhd,kd->hqk", grad_att, values_ext, preferred_element_type=jnp.float32)
    inner_sum = jnp.sum(attn_prob * grad_prob, axis=-1, keepdims=True)
    grad_scores = (attn_prob * (grad_prob - inner_sum)).astype(jnp.bfloat16)
    grad_query = (
        jnp.einsum("hqk,kd->qhd", grad_scores, keys_ext, preferred_element_type=jnp.float32)
        * score_scale
    )
    grad_keys_ext = (
        jnp.einsum("hqk,qhd->kd", grad_scores, query_low, preferred_element_type=jnp.float32)
        * score_scale
    )
    grad_values_ext = jnp.einsum(
        "hqk,qhd->kd", attn_prob.astype(jnp.bfloat16), grad_att, preferred_element_type=jnp.float32
    )
    grad_pairs = jnp.concatenate([grad_keys_ext, grad_values_ext], axis=1)
    own_grad = grad_pairs[hop_count * tokens :]
    for distance in range(1, hop_count + 1):
        lower_row = (hop_count - distance) * tokens
        own_grad = own_grad + shifted(grad_pairs[lower_row : lower_row + tokens], "seq", -distance)
    _, back_turn = jax.vjp(turn_norm, query_raw, key_raw, query_gain, key_gain)
    grad_qraw, grad_kraw, grad_qgain, grad_kgain = back_turn((grad_query, own_grad[:, :head_width]))
    grad_raw = jnp.concatenate(
        [
            grad_qraw.astype(jnp.bfloat16),
            grad_kraw.astype(jnp.bfloat16),
            own_grad[:, head_width:].astype(jnp.bfloat16),
        ],
        axis=1,
    )
    into_grad = row_outer(normed, grad_raw)
    grad_normed = back_product(grad_raw, into_w)
    _, back_pre1 = jax.vjp(rms_scale, source, attn_gain)
    grad_source, grad_pre1 = back_pre1(grad_normed)
    grad_input = grad_mid + grad_source
    grads = [
        grad.astype(jnp.bfloat16).reshape(size, -1, grad.shape[-1])
        for grad in (into_grad, output_grad, ffn_grad, down_grad)
    ]
    local = (grad_pre1, grad_post1, grad_pre2, grad_post2, grad_qgain, grad_kgain)
    gain_grads = pack_gains([member.reshape(size, -1) for member in local], 8)
    piece_widths = [[shards[member].shape[1] for member in group] for group in groups]
    *results, gain_total = reduce_grads(grads, piece_widths, by_rows, shared, gain_grads)
    return (
        result.astype(jnp.bfloat16)[None],
        grad_input.astype(jnp.bfloat16)[None],
        *results,
        *unpack_gains(gain_total, widths),
    )


def solution(mesh):
    placed = (
        P("fsdp", "seq", None),
        P("fsdp", "seq", None),
        P("fsdp", None),
        P("fsdp", None),
        P("fsdp", None),
        P("fsdp", None),
        P("fsdp", None),
        P("fsdp", None),
        P("fsdp", None),
        P("fsdp"),
        P("fsdp"),
        P("fsdp"),
        P("fsdp"),
        P("fsdp"),
        P("fsdp"),
    )
    return jax.shard_map(
        on_device,
        mesh=mesh,
        in_specs=placed,
        out_specs=(
            P("fsdp", "seq", None),
            P("fsdp", "seq", None),
            P("fsdp", None),
            P("fsdp", None),
            P("fsdp", None),
            P("fsdp", None),
            P("fsdp", None),
            P("fsdp", None),
            P("fsdp", None),
            P("fsdp"),
            P("fsdp"),
            P("fsdp"),
            P("fsdp"),
            P("fsdp"),
            P("fsdp"),
        ),
        check_vma=False,
    )
```
